128 devices in a mesh: section: 2 (over y_hi), shard: 2 (over core), replica: 32 (over y_lo, z, x).
Axes of the slice: x: 4, y: 4 (y_hi: 2, y_lo: 2; y = y_hi * 2 + y_lo), z: 4, core: 2. Of those that a mesh axis runs over, the one named last changes fastest.
Arguments:
- inputs: bfloat16 [2, 64, 128, 1024], P(None, ('shard', 'replica')), may hold values from -6 to 6
- cotangent: bfloat16 [2, 64, 128, 1024], P(None, ('shard', 'replica')), may hold values from -6 to 6
- segments: int32 [2, 64, 128], P(None, ('shard', 'replica')), may hold values from 0 to 3, never falling along the last dimension, each value on 1 to 64 neighbouring positions
- routes: int32 [2, 2, 64, 128, 2], P('section', None, ('shard', 'replica')), may hold values from 0 to 2, all different within a row; in each aligned block of 128 rows (0 to 127, 128 to 255, ..., all dimensions but the last counted through in order) at most 96 rows name the same one
- mixer_gain: bfloat16 [2, 1024], P('section', 'shard'), may hold values from 0.5 to 1.5
- query_weight: bfloat16 [2, 1024, 1024], P('section', 'shard'), may hold values from -0.25 to 0.25
- key_matrix: bfloat16 [2, 1024, 512], P('section', 'shard'), may hold values from -0.25 to 0.25
- value_matrix: bfloat16 [2, 1024, 512], P('section', 'shard'), may hold values from -0.1875 to 0.1875
- out_weight: bfloat16 [2, 1024, 1024], P('section', 'shard'), may hold values from -0.375 to 0.375
- expert_gain: bfloat16 [2, 1024], P('section', 'shard'), may hold values from 0.5 to 1.5
- router_weight: bfloat16 [2, 1024, 3], P('section', 'shard'), may hold values from -0.125 to 0.125
- gate_weight: bfloat16 [2, 3, 1024, 512], P('section', None, 'shard'), may hold values from -0.1875 to 0.1875
- up_weight: bfloat16 [2, 3, 1024, 512], P('section', None, 'shard'), may hold values from -0.1875 to 0.1875
- down_weight: bfloat16 [2, 3, 512, 1024], P('section', None, 'shard'), may hold values from -0.5 to 0.5
Outputs:
- section_output: float32 [2, 2, 64, 128, 1024], P('section', None, ('shard', 'replica'))
- input_gradient: float32 [2, 2, 64, 128, 1024], P('section', None, ('shard', 'replica'))
- mixer_gain_gradient: float32 [2, 1024], P('section', 'shard')
- query_weight_gradient: float32 [2, 1024, 1024], P('section', 'shard')
- key_weight_gradient: float32 [2, 1024, 512], P('section', 'shard')
- value_weight_gradient: float32 [2, 1024, 512], P('section', 'shard')
- out_weight_gradient: float32 [2, 1024, 1024], P('section', 'shard')
- expert_gain_gradient: float32 [2, 1024], P('section', 'shard')
- router_weight_gradient: float32 [2, 1024, 3], P('section', 'shard')
- gate_weight_gradient: float32 [2, 3, 1024, 512], P('section', None, 'shard')
- up_weight_gradient: float32 [2, 3, 1024, 512], P('section', None, 'shard')
- down_weight_gradient: float32 [2, 3, 512, 1024], P('section', None, 'shard')
The draws below stay inside these ranges and needn't reach their ends.
Inputs may be any that keep to these rules, and one draw needn't show every extreme that they name: `segments`: segment numbers never fall along a packed sequence; one segment spans half of 128 tokens. `routes`: each token names 2 different experts; within one packed sequence of one micro-batch and section, no expert is named by more than 96 tokens, a bound that some block reaches.
All inputs are finite; a program needn't handle non-finite values.
Results may differ from the reference program's by a relative error of at most 0.04.
Values may be sent and summed in bfloat16 or wider, within the bound.
A program may use at most 192 MiB of HBM per device.

```python
import math
import jax
import jax.numpy as jnp
import numpy as np
from jax import lax

MODEL_WIDTH = 1024
QUERY_HEADS = 16
KEY_VALUE_HEADS = 8
HEAD_SIZE = 64
FF = 512
E = 3
TOPK = 2
MB = 2
SEQ = 128
CAP = 96
PACKS = 64
N_SECTION = 2


def levels(stream_key, shape, shards, low, largest):
    gain = 1.0
    for axis_at, shards_of in shards:
        heights = jax.random.uniform(jax.random.fold_in(jax.random.fold_in(stream_key, 6), axis_at), (shards_of,), jnp.float32, low / len(shards), largest / len(shards))
        gain = gain * jnp.repeat(jnp.exp(heights), shape[axis_at] // shards_of).reshape((-1,) + (1,) * (len(shape) - 1 - axis_at))
    return gain


def split_up(count, total, limit, slope):
    weights = [(1 << 20) // math.isqrt(grade ** slope) + 1 for grade in range(2, count + 1)]
    spare, holding = total - limit - (count - 1), [1] * (count - 1)
    while spare > 0:
        movable = [i for i in range(count - 1) if holding[i] < limit]
        whole, left = sum([weights[i] for i in movable]), spare
        for i in movable:
            extra = min(limit - holding[i], max(1, left * weights[i] // whole), spare)
            holding[i] = holding[i] + extra
            spare = spare - extra
    return np.array([limit] + holding)


def ragged_sizes(key, amount, total, reach, skew):
    if amount == 2:
        one = jax.random.randint(key, (), max(1, total - reach), min(reach, total - 1) + 1)
        return jnp.stack([one, total - one])
    tallies = jnp.asarray(split_up(amount, total, reach, skew), jnp.int32)
    twos = (amount - 1) // 2
    giver, receiver = tallies[1:1 + 2 * twos:2], tallies[2:2 + 2 * twos:2]
    slack = jnp.minimum(giver - 1, reach - receiver)
    shifted = jax.random.randint(jax.random.fold_in(key, 1), (twos,), 0, 1 << 20) % (slack + 1)
    tallies = tallies.at[1:1 + 2 * twos:2].set(giver - shifted).at[2:2 + 2 * twos:2].set(receiver + shifted)
    return tallies[jax.random.permutation(jax.random.fold_in(key, 2), amount)]


def shared_out(rng, own, number, rows, amount, top, reach, skew):
    order = jax.random.permutation(rng, amount)
    packed, common = portions_of(amount, rows * top, reach, skew, True), portions_of(amount, rows * top, reach, skew, False)
    places = jnp.arange(amount)

    def named(sizes, offset_by):
        used = int((sizes > 0).sum())
        fixed = max(1, used // 4)
        moved = fixed + (places - fixed + offset_by * (used - fixed)) % max(1, amount - fixed)
        return jnp.zeros((amount,), jnp.int32).at[order[jnp.where(places < fixed, places, moved)]].set(jnp.asarray(sizes, jnp.int32))

    sizes = jnp.where(number % 4 == 0, named(packed, number // 4), named(common, number - number // 4 - 1))
    mixed = jax.random.permutation(jax.random.fold_in(own, 3), amount)
    source_of, receiver = mixed[0:amount // 2 * 2:2], mixed[1:amount // 2 * 2:2]
    room = jnp.minimum(sizes[source_of] - 1, reach - sizes[receiver]) // 2
    room = jnp.where((source_of == order[0]) | (receiver == order[0]) | (sizes[receiver] == 0), 0, jnp.maximum(room, 0))
    moved = jax.random.randint(jax.random.fold_in(own, 4), (amount // 2,), 0, 1 << 20) % (room + 1)
    sizes = sizes.at[source_of].add(-moved).at[receiver].add(moved)
    items = jnp.searchsorted(jnp.cumsum(sizes), jnp.arange(rows * top), side="right").astype(jnp.int32)
    grid = items.reshape(top, rows).T
    grid = grid[jax.random.permutation(jax.random.fold_in(own, 1), rows)]
    offset_by = jax.random.randint(jax.random.fold_in(own, 2), (rows, 1), 0, top)
    return jnp.take_along_axis(grid, (jnp.arange(top)[None, :] + offset_by) % top, axis=1)


def portions_of(count, total, most, lean, full):
    loads = [(1 << 20) // math.isqrt(grade ** lean) + 1 for grade in range(1, count + 1)]
    largest = most if full else min(most, max(-(-total // count), total * loads[0] // sum(loads)))
    least = 1 if total - largest >= count - 1 else 0
    holding, spare = [largest] + [least] * (count - 1), total - largest - least * (count - 1)
    while spare > 0:
        movable = [i for i in range(1, count) if holding[i] < largest] or [i for i in range(1, count) if holding[i] < most]
        mass, left = sum([loads[i] for i in movable]), spare
        for i in movable:
            more = min(most - holding[i], max(1, left * loads[i] // mass), spare)
            holding[i] = holding[i] + more
            spare = spare - more
    return np.array(holding)


def noise(own_key, shape, deviation, reach, cuts=(), kind=jnp.bfloat16):
    entries = jax.random.normal(own_key, shape, jnp.float32) * deviation
    if len(cuts) > 0:
        entries = levels(own_key, shape, cuts, -0.22, 0.18) * entries
    return jnp.clip(entries, min=-reach, max=reach).astype(kind)


def setup_inputs(seed: int = 0) -> dict:
    arg_keys = jax.random.split(jax.random.key(seed), 15)
    inputs = noise(arg_keys[0], (MB, PACKS, SEQ, MODEL_WIDTH), 1.0, 6.0, ((1, 64),))
    cotangent = noise(arg_keys[1], (MB, PACKS, SEQ, MODEL_WIDTH), 1.0, 6.0, ((1, 64),))
    segments = jax.vmap(lambda own: jnp.searchsorted(jnp.cumsum(ragged_sizes(own, 4, SEQ, SEQ // 2, 0)), jnp.arange(SEQ), side="right"))(jax.random.split(arg_keys[2], MB * PACKS)).reshape((MB, PACKS, SEQ)).astype(jnp.int32)
    routes_keys = jax.random.split(jax.random.fold_in(arg_keys[3], 1), N_SECTION * MB * PACKS * SEQ // SEQ)
    routes_turns = jax.random.permutation(jax.random.fold_in(arg_keys[3], 3), N_SECTION * MB * PACKS * SEQ // SEQ)
    routes = jax.vmap(lambda own, number: shared_out(jax.random.fold_in(arg_keys[3], 2), own, number, SEQ, E, TOPK, CAP, 1))(routes_keys, routes_turns).reshape((N_SECTION, MB, PACKS, SEQ, TOPK))
    mixer_gain = jnp.clip(1.0 + 0.1 * jax.random.normal(arg_keys[4], (N_SECTION, MODEL_WIDTH), jnp.float32), 0.5, 1.5).astype(jnp.bfloat16)
    query_weight = noise(arg_keys[5], (N_SECTION, MODEL_WIDTH, QUERY_HEADS * HEAD_SIZE), (MODEL_WIDTH // 2) ** -0.5, 0.25, ((0, 2), (1, 2)))
    key_matrix = noise(arg_keys[6], (N_SECTION, MODEL_WIDTH, KEY_VALUE_HEADS * HEAD_SIZE), (MODEL_WIDTH // 2) ** -0.5, 0.25, ((0, 2), (1, 2)))
    value_matrix = noise(arg_keys[7], (N_SECTION, MODEL_WIDTH, KEY_VALUE_HEADS * HEAD_SIZE), MODEL_WIDTH ** -0.5, 0.1875, ((0, 2), (1, 2)))
    out_weight = noise(arg_keys[8], (N_SECTION, QUERY_HEADS * HEAD_SIZE, MODEL_WIDTH), (QUERY_HEADS * HEAD_SIZE // 4) ** -0.5, 0.375, ((0, 2), (1, 2)))
    expert_gain = jnp.clip(1.0 + 0.1 * jax.random.normal(arg_keys[9], (N_SECTION, MODEL_WIDTH), jnp.float32), 0.5, 1.5).astype(jnp.bfloat16)
    router_weight = noise(arg_keys[10], (N_SECTION, MODEL_WIDTH, E), (2 * MODEL_WIDTH) ** -0.5, 0.125, ((0, 2), (1, 2)))
    gate_weight = noise(arg_keys[11], (N_SECTION, E, MODEL_WIDTH, FF), MODEL_WIDTH ** -0.5, 0.1875, ((0, 2), (2, 2)))
    up_weight = noise(arg_keys[12], (N_SECTION, E, MODEL_WIDTH, FF), MODEL_WIDTH ** -0.5, 0.1875, ((0, 2), (2, 2)))
    down_weight = noise(arg_keys[13], (N_SECTION, E, FF, MODEL_WIDTH), (FF // 4) ** -0.5, 0.5, ((0, 2), (2, 2)))
    return {"inputs": inputs, "cotangent": cotangent, "segments": segments, "routes": routes, "mixer_gain": mixer_gain, "query_weight": query_weight, "key_matrix": key_matrix, "value_matrix": value_matrix, "out_weight": out_weight, "expert_gain": expert_gain, "router_weight": router_weight, "gate_weight": gate_weight, "up_weight": up_weight, "down_weight": down_weight}


epsilon = 1e-06
highest = lax.Precision.HIGHEST

@jax.custom_vjp
def lower_bound(v):
    return lax.optimization_barrier(v.astype(jnp.bfloat16)).astype(jnp.float32)

@jax.custom_vjp
def low_back(v):
    return v

def low_keep(v):
    return (lower_bound(v), None)

def low_pass(kept, grad):
    return (grad,)

def back_keep(v):
    return (v, None)

def back_low(kept, grad):
    return (lower_bound(grad),)
lower_bound.defvjp(low_keep, low_pass)
low_back.defvjp(back_keep, back_low)

def norm_scale(hidden):
    return lax.rsqrt(lax.optimization_barrier(jnp.mean(hidden * hidden, axis=-1, keepdims=True)) + epsilon)

def rotary_tables(sequence_length, width):
    half = width // 2
    frequency = jnp.power(10000.0, -2.0 * jnp.arange(half, dtype=jnp.float32) / width)
    angles = jnp.arange(sequence_length, dtype=jnp.float32)[:, None] * frequency[None, :]
    cosine_table = jnp.concatenate([jnp.cos(angles), jnp.cos(angles)], axis=-1)[:, None, :]
    sine_table = jnp.concatenate([jnp.sin(angles), jnp.sin(angles)], axis=-1)[:, None, :]
    return (cosine_table, sine_table)

def rotate_halves(value_rows, cosine_table, sine_table):
    half = value_rows.shape[-1] // 2
    turned = jnp.concatenate([-value_rows[..., half:], value_rows[..., :half]], axis=-1)
    return value_rows * cosine_table + turned * sine_table

def slot_targets(routes):
    shape = routes.shape
    flat = routes.reshape(shape[:-2] + (shape[-2] * shape[-1],))
    marks = (flat[..., None] == jnp.arange(E, dtype=jnp.int32)).astype(jnp.int32)
    before = (jnp.cumsum(marks, axis=-2) - marks).astype(jnp.int32)
    slots = lax.optimization_barrier(jnp.sum(before * marks, axis=-1)).astype(jnp.int32)
    return (flat * CAP + slots).astype(jnp.int32).reshape(shape)

def layer(hidden, segments, routes, weights):
    mixer_gain, query_weight, key_matrix, value_matrix, out_weight, expert_gain, router_weight, gate_weight, up_weight, down_weight = weights
    packed_groups, sequence_length = (hidden.shape[0], hidden.shape[1])
    repeat_factor = QUERY_HEADS // KEY_VALUE_HEADS
    cosine_table, sine_table = rotary_tables(sequence_length, HEAD_SIZE)
    normalized_input = lower_bound(hidden * norm_scale(hidden) * mixer_gain)
    query_rows = low_back(jnp.einsum('psd,de->pse', normalized_input, query_weight, precision=highest))
    query_rows = lower_bound(rotate_halves(query_rows.reshape(packed_groups, sequence_length, QUERY_HEADS, HEAD_SIZE), cosine_table, sine_table))
    query_rows = query_rows.reshape(packed_groups, sequence_length, KEY_VALUE_HEADS, repeat_factor, HEAD_SIZE)
    key_rows = low_back(jnp.einsum('psd,de->pse', normalized_input, key_matrix, precision=highest))
    key_rows = lower_bound(rotate_halves(key_rows.reshape(packed_groups, sequence_length, KEY_VALUE_HEADS, HEAD_SIZE), cosine_table, sine_table))
    value_rows = low_back(lower_bound(jnp.einsum('psd,de->pse', normalized_input, value_matrix, precision=highest)))
    value_rows = value_rows.reshape(packed_groups, sequence_length, KEY_VALUE_HEADS, HEAD_SIZE)
    raw = low_back(jnp.einsum('pqgrd,pkgd->pgrqk', query_rows, key_rows, precision=highest))
    places = jnp.arange(sequence_length, dtype=jnp.int32)
    allowed = (segments[:, :, None] == segments[:, None, :]) & (places[None, None, :] <= places[None, :, None])
    scores = jnp.where(allowed[:, None, None], raw * (1.0 / math.sqrt(HEAD_SIZE)), -1e+30)
    top = lax.optimization_barrier(jnp.max(scores, axis=-1, keepdims=True))
    exponent = jnp.exp(scores - top)
    attention = exponent / lax.optimization_barrier(jnp.sum(exponent, axis=-1, keepdims=True))
    attended = jnp.einsum('pgrqk,pkgd->pqgrd', lower_bound(attention), value_rows, precision=highest)
    attended = low_back(lower_bound(attended.reshape(packed_groups, sequence_length, QUERY_HEADS * HEAD_SIZE)))
    middle = hidden + low_back(jnp.einsum('pse,ed->psd', attended, out_weight, precision=highest))
    normed_expert = lower_bound(middle * norm_scale(middle) * expert_gain)
    logits = low_back(jnp.einsum('psd,de->pse', normed_expert, router_weight, precision=highest))
    route_hot = (routes[..., None] == jnp.arange(E, dtype=jnp.int32)).astype(jnp.float32)
    chosen = lax.optimization_barrier(jnp.sum(route_hot * logits[:, :, None, :], axis=-1))
    chosen_peak = lax.optimization_barrier(jnp.max(chosen, axis=-1, keepdims=True))
    lifted = jnp.exp(chosen - chosen_peak)
    gates = lifted / lax.optimization_barrier(jnp.sum(lifted, axis=-1, keepdims=True))
    slot_hot = (slot_targets(routes)[..., None] == jnp.arange(E * CAP, dtype=jnp.int32)).astype(jnp.float32)
    dispatched = low_back(jnp.einsum('pskc,psd->pcd', slot_hot, normed_expert, precision=highest))
    dispatched = dispatched.reshape(packed_groups, E, CAP, MODEL_WIDTH)
    gate_linear = low_back(jnp.einsum('pecd,edf->pecf', dispatched, gate_weight, precision=highest))
    up_linear = low_back(jnp.einsum('pecd,edf->pecf', dispatched, up_weight, precision=highest))
    inner = lower_bound(jax.nn.silu(gate_linear) * up_linear)
    expert_out = low_back(lower_bound(jnp.einsum('pecf,efd->pecd', inner, down_weight, precision=highest)))
    expert_out = expert_out.reshape(packed_groups, E * CAP, MODEL_WIDTH)
    picked = jnp.einsum('pskc,pcd->pskd', slot_hot, expert_out, precision=highest)
    return middle + lax.optimization_barrier(jnp.sum(gates[..., None] * picked, axis=2))

def group_count(total, sequence_length):
    size = 1
    for candidate in range(1, total + 1):
        if total % candidate == 0 and candidate * sequence_length <= 4096:
            size = candidate
    return size

def apply_section(hidden, segments, routes, weights):
    total = hidden.shape[0]
    size = group_count(total, SEQ)
    count = total // size

    def one_group(item):
        return layer(item[0], item[1], item[2], weights)
    grouped = (hidden.reshape(count, size, SEQ, MODEL_WIDTH), segments.reshape(count, size, SEQ), routes.reshape(count, size, SEQ, TOPK))
    result = lax.map(jax.checkpoint(one_group), grouped)
    return result.reshape(total, SEQ, MODEL_WIDTH)

def reference(inputs, cotangent, segments, routes, mixer_gain, query_weight, key_matrix, value_matrix, out_weight, expert_gain, router_weight, gate_weight, up_weight, down_weight):
    weights = (mixer_gain, query_weight, key_matrix, value_matrix, out_weight, expert_gain, router_weight, gate_weight, up_weight, down_weight)
    total = MB * PACKS
    flat_inputs = inputs.astype(jnp.float32).reshape(total, SEQ, MODEL_WIDTH)
    flat_segments = segments.reshape(total, SEQ)
    flat_routes = routes.reshape(N_SECTION, total, SEQ, TOPK)
    first_weights = tuple((item[0].astype(jnp.float32) for item in weights))
    second_weights = tuple((item[1].astype(jnp.float32) for item in weights))

    def forward(start, joined, weights_first, weights_second):
        first_out = apply_section(start, flat_segments, flat_routes[0], weights_first)
        sent = low_back(lower_bound(first_out)) + joined
        return (first_out, apply_section(sent, flat_segments, flat_routes[1], weights_second))
    outputs, pullback = jax.vjp(forward, flat_inputs, jnp.zeros_like(flat_inputs), first_weights, second_weights)
    grads = pullback((jnp.zeros_like(flat_inputs), cotangent.astype(jnp.float32).reshape(total, SEQ, MODEL_WIDTH)))
    shape = (N_SECTION, MB, PACKS, SEQ, MODEL_WIDTH)
    section_output = jnp.stack([outputs[0], outputs[1]]).reshape(shape)
    input_gradient = jnp.stack([grads[0], grads[1]]).reshape(shape)
    stacked = tuple((jnp.stack([grads[2][index], grads[3][index]]) for index in range(10)))
    return (section_output, input_gradient, stacked[0], stacked[1], stacked[2], stacked[3], stacked[4], stacked[5], stacked[6], stacked[7], stacked[8], stacked[9])
```

```python
import functools

import numpy as np
import jax
import jax.numpy as jnp
from jax import lax
from jax.experimental import pallas as pl
from jax.experimental.pallas import tpu as pltpu
from jax.sharding import PartitionSpec as P

MESH = pl.DeviceIdType.MESH
ROWS = 7680
COLS = 512
PARTS = 5
PART = ROWS // PARTS
DIMS = 5


def cube_position():
    r = lax.axis_index("replica")
    x = r % 4
    z = (r // 4) % 4
    y = r // 16
    bits = (((x + 1) // 2) % 2, x // 2, ((z + 1) // 2) % 2, z // 2, y)
    partners = (
        r + 1 - 2 * (x % 2),
        r + 3 - 2 * x,
        r + 4 - 8 * (z % 2),
        r + 12 - 8 * z,
        (r + 16) % 32,
    )
    return bits, partners


def add_rows(dst, dst_at, a, a_at, b, b_at, count):
    step = min(count, 192)

    def one(i, carry):
        at = i * step
        dst[pl.ds(pl.multiple_of(dst_at + at, 16), step), :] = (
            a[pl.ds(pl.multiple_of(a_at + at, 16), step), :]
            + b[pl.ds(pl.multiple_of(b_at + at, 16), step), :]
        )
        return carry

    lax.fori_loop(0, count // step, one, 0)


def reduce_kernel(
    parts_ref, small_ref, out_ref, small_out,
    work, from_core, from_cube, whole, small_held, small_got,
    load_sem, core_send, core_recv, cube_send, cube_recv,
    share_send, share_recv, small_send, small_recv, store_sem,
):
    core = lax.axis_index("shard")
    bits, partners = cube_position()
    sibling = {"shard": 1 - core}

    barrier = pltpu.get_barrier_semaphore()
    pl.semaphore_signal(barrier, inc=1, device_id=sibling, device_id_type=MESH)
    for partner in partners:
        pl.semaphore_signal(barrier, inc=1, device_id={"replica": partner}, device_id_type=MESH)

    loads = []
    for p in range(PARTS):
        load = pltpu.make_async_copy(
            parts_ref.at[core, pl.ds(p * PART, PART)], work.at[pl.ds(p * PART, PART)], load_sem.at[p]
        )
        load.start()
        loads.append(load)
    pl.semaphore_wait(barrier, 1 + DIMS)

    cores = []
    small_core = pltpu.make_async_remote_copy(
        src_ref=small_ref.at[1 - core], dst_ref=small_got.at[0],
        send_sem=small_send.at[0], recv_sem=small_recv.at[0],
        device_id=sibling, device_id_type=MESH,
    )
    small_core.start()
    for p in range(PARTS):
        copy = pltpu.make_async_remote_copy(
            src_ref=parts_ref.at[1 - core, pl.ds(p * PART, PART)],
            dst_ref=from_core.at[pl.ds(p * PART, PART)],
            send_sem=core_send.at[p], recv_sem=core_recv.at[p],
            device_id=sibling, device_id_type=MESH,
        )
        copy.start()
        cores.append(copy)

    sends = [small_core] + cores
    kept = [0] * PARTS

    def start_scatter(p, s):
        d = (p + s) % DIMS
        size = PART >> (s + 1)
        slot = p * PART + PART - (PART >> s)
        away = kept[p] + (1 - bits[d]) * size
        kept[p] = kept[p] + bits[d] * size
        copy = pltpu.make_async_remote_copy(
            src_ref=work.at[pl.ds(pl.multiple_of(p * PART + away, 16), size)],
            dst_ref=from_cube.at[pl.ds(slot, size)],
            send_sem=cube_send.at[p * DIMS + s], recv_sem=cube_recv.at[p * DIMS + s],
            device_id={"replica": partners[d]}, device_id_type=MESH,
        )
        copy.start()
        sends.append(copy)
        return copy

    def start_small(s):
        copy = pltpu.make_async_remote_copy(
            src_ref=small_held.at[s], dst_ref=small_got.at[s + 1],
            send_sem=small_send.at[s + 1], recv_sem=small_recv.at[s + 1],
            device_id={"replica": partners[s]}, device_id_type=MESH,
        )
        copy.start()
        sends.append(copy)
        return copy

    def start_share(p, s):
        d = (p + s) % DIMS
        size = PART >> (s + 1)
        copy = pltpu.make_async_remote_copy(
            src_ref=whole.at[pl.ds(pl.multiple_of(p * PART + kept[p], 16), size)],
            dst_ref=whole.at[pl.ds(pl.multiple_of(p * PART + kept[p], 16), size)],
            send_sem=share_send.at[p * DIMS + s], recv_sem=share_recv.at[p * DIMS + s],
            device_id={"replica": partners[d]}, device_id_type=MESH,
        )
        copy.start()
        sends.append(copy)
        return copy

    stores = []

    def start_store(at, size, index):
        copy = pltpu.make_async_copy(
            whole.at[pl.ds(pl.multiple_of(at, 16), size)],
            out_ref.at[pl.ds(pl.multiple_of(at, 16), size)],
            store_sem.at[index],
        )
        copy.start()
        stores.append(copy)

    cube = [None] * PARTS
    for p in range(PARTS):
        loads[p].wait()
        cores[p].wait_recv()
        add_rows(work, p * PART, work, p * PART, from_core, p * PART, PART)
        cube[p] = start_scatter(p, 0)
    small_core.wait_recv()
    small_held[0] = small_ref[core] + small_got[0]
    small = start_small(0)

    share = [None] * PARTS
    for s in range(DIMS):
        for p in range(PARTS):
            cube[p].wait_recv()
            size = PART >> (s + 1)
            slot = p * PART + PART - (PART >> s)
            at = p * PART + kept[p]
            last = s == DIMS - 1
            add_rows(whole if last else work, at, work, at, from_cube, slot, size)
            if last:
                share[p] = start_share(p, s)
                start_store(at, size, p)
            else:
                cube[p] = start_scatter(p, s + 1)
        small.wait_recv()
        if s < DIMS - 1:
            small_held[s + 1] = small_held[s] + small_got[s + 1]
            small = start_small(s + 1)
        else:
            small_out[...] = small_held[s] + small_got[s + 1]

    for s in reversed(range(DIMS)):
        for p in range(PARTS):
            d = (p + s) % DIMS
            size = PART >> (s + 1)
            share[p].wait_recv()
            got = kept[p] + size - 2 * bits[d] * size
            kept[p] = kept[p] - bits[d] * size
            if s > 0:
                share[p] = start_share(p, s - 1)
            start_store(p * PART + got, size, PARTS + p * DIMS + s)

    for copy in sends:
        copy.wait_send()
    for copy in stores:
        copy.wait()


def reduce_gradients(parts, small):
    dma = pltpu.SemaphoreType.DMA
    return pl.pallas_call(
        reduce_kernel,
        out_shape=(
            jax.ShapeDtypeStruct((ROWS, COLS), jnp.bfloat16),
            jax.ShapeDtypeStruct((16, COLS), jnp.float32),
        ),
        in_specs=[pl.BlockSpec(memory_space=pl.ANY), pl.BlockSpec(memory_space=pltpu.VMEM)],
        out_specs=(pl.BlockSpec(memory_space=pl.ANY), pl.BlockSpec(memory_space=pltpu.VMEM)),
        scratch_shapes=[
            pltpu.VMEM((ROWS, COLS), jnp.bfloat16),
            pltpu.VMEM((ROWS, COLS), jnp.bfloat16),
            pltpu.VMEM((ROWS, COLS), jnp.bfloat16),
            pltpu.VMEM((ROWS, COLS), jnp.bfloat16),
            pltpu.VMEM((DIMS, 16, COLS), jnp.float32),
            pltpu.VMEM((DIMS + 1, 16, COLS), jnp.float32),
            dma((PARTS,)), dma((PARTS,)), dma((PARTS,)),
            dma((PARTS * DIMS,)), dma((PARTS * DIMS,)),
            dma((PARTS * DIMS,)), dma((PARTS * DIMS,)),
            dma((DIMS + 1,)), dma((DIMS + 1,)),
            dma((PARTS + PARTS * DIMS,)),
        ],
        compiler_params=pltpu.CompilerParams(
            collective_id=1, has_side_effects=True, vmem_limit_bytes=48 * 1024 * 1024
        ),
    )(parts, small)


def gather_kernel(count, *refs):
    mine, others = refs[:count], refs[count:2 * count]
    send_sem, recv_sem = refs[2 * count:]
    sibling = {"shard": 1 - lax.axis_index("shard")}
    barrier = pltpu.get_barrier_semaphore()
    pl.semaphore_signal(barrier, inc=1, device_id=sibling, device_id_type=MESH)
    pl.semaphore_wait(barrier, 1)
    copies = []
    for i in range(count):
        copy = pltpu.make_async_remote_copy(
            src_ref=mine[i], dst_ref=others[i],
            send_sem=send_sem.at[i], recv_sem=recv_sem.at[i],
            device_id=sibling, device_id_type=MESH,
        )
        copy.start()
        copies.append(copy)
    for copy in copies:
        copy.wait()


def exchange(*arrays):
    n = len(arrays)
    return pl.pallas_call(
        functools.partial(gather_kernel, n),
        out_shape=tuple(jax.ShapeDtypeStruct(a.shape, a.dtype) for a in arrays),
        in_specs=[pl.BlockSpec(memory_space=pl.ANY)] * n,
        out_specs=tuple(pl.BlockSpec(memory_space=pl.ANY) for _ in arrays),
        scratch_shapes=[pltpu.SemaphoreType.DMA((n,)), pltpu.SemaphoreType.DMA((n,))],
        compiler_params=pltpu.CompilerParams(collective_id=2, has_side_effects=True),
    )(*arrays)


EPSILON = 1e-06
WEIGHT_SHAPES = (
    (1024, 1024), (1024, 512), (1024, 512), (1024, 1024), (3, 1024, 512), (3, 1024, 512), (3, 512, 1024),
)
NT = (((1,), (1,)), ((), ()))
NN = (((1,), (0,)), ((), ()))
TN = (((0,), (0,)), ((), ()))
F32 = jnp.float32
BF16 = jnp.bfloat16
TOKENS = 256
WIDTH = 1024
VMEM_LIMIT = 56 * 1024 * 1024


def dot(a, b, dims):
    return lax.dot_general(a, b, dims, preferred_element_type=F32)


def weight_copies(mine, others, held, sems):
    core = lax.axis_index("shard")
    copies = []
    for i, (a, b, w) in enumerate(zip(mine, others, held)):
        rows = a.shape[-2]
        axis = len(a.shape) - 2
        pair = []
        for j, (source, owner) in enumerate(((a, core), (b, 1 - core))):
            place = pl.ds(pl.multiple_of(owner * rows, rows), rows)
            target = w.at[place] if axis == 0 else w.at[:, place]
            pair.append(pltpu.make_async_copy(source, target, sems.at[2 * i + j]))
        copies.append(pair)
    return copies


def start_all(copies, order):
    for i in order:
        for copy in copies[i]:
            copy.start()


def arrive(copies, *which):
    for i in which:
        for copy in copies[i]:
            copy.wait()


def small_rows(mine, other):
    first = lax.axis_index("shard") == 0
    a, b = mine[...], other[...]
    return jnp.concatenate([jnp.where(first, a, b), jnp.where(first, b, a)], axis=1)


def scale_of(rows):
    return lax.rsqrt(jnp.mean(rows * rows, axis=-1, keepdims=True) + EPSILON)


def swap_halves(u):
    lanes = u.shape[1]
    lane = lax.broadcasted_iota(jnp.int32, u.shape, 1)
    return jnp.where(lane % 64 < 32, pltpu.roll(u, lanes - 32, 1), pltpu.roll(u, 32, 1))


def low_half(shape):
    return lax.broadcasted_iota(jnp.int32, shape, 1) < 64


def both_ways(block):
    wide = block.astype(F32)
    turned = pltpu.roll(wide, 64, 1)
    low = low_half(wide.shape)
    return jnp.where(low, wide, turned).astype(BF16), jnp.where(low, turned, wide).astype(BF16)


def stack_heads(block):
    wide = block.astype(F32)
    low = low_half(wide.shape)
    zero = jnp.zeros_like(wide)
    return jnp.concatenate([jnp.where(low, wide, zero), jnp.where(low, zero, wide)], axis=0).astype(BF16)


def join_heads(rows):
    return jnp.where(low_half((128, 128)), rows[:128], rows[128:])


def forward_kernel(
    start_ref, received_ref, bias_ref, marks_ref, cos_ref, sin_ref, small_mine, small_other, *refs
):
    mine, others, refs = refs[:7], refs[7:14], refs[14:]
    (relay_ref, out_ref, hidden_ref, normed_ref, q_ref, k_ref, v_ref, p_ref, att_ref, middle_ref, ne_ref,
     gates_ref, gl_ref, ul_ref, gi_ref) = refs[:15]
    held, sems = refs[15:22], refs[22]
    wq, wk, wv, wo, wg, wu, wd = held
    copies = weight_copies(mine, others, held, sems)
    start_all(copies, range(7))
    small = small_rows(small_mine, small_other)
    first = lax.axis_index("section") == 0
    hidden = jnp.where(first, start_ref[...], received_ref[...])
    hidden_ref[...] = hidden
    x = hidden.astype(F32)
    normed_ref[...] = (x * scale_of(x) * small[0:1].astype(F32)).astype(BF16)

    def block(ref, i, size=256):
        return ref[:, i * size:(i + 1) * size]

    for weight, target, number, turned, index in (
        (wq, q_ref, 4, True, 0), (wk, k_ref, 2, True, 1), (wv, v_ref, 2, False, 2),
    ):
        arrive(copies, index)
        for i in range(number):
            u = dot(normed_ref[...], block(weight, i), NN)
            if turned:
                u = u * cos_ref[...] + swap_halves(u) * sin_ref[...]
            target[:, i * 256:(i + 1) * 256] = u.astype(BF16)

    for pack in range(2):
        rows = slice(pack * 128, pack * 128 + 128)
        bias = bias_ref[pack]
        bias = jnp.concatenate([bias, bias], axis=0)
        for pair in range(4):
            keys = both_ways(k_ref[rows, pair * 128:(pair + 1) * 128])
            values = both_ways(v_ref[rows, pair * 128:(pair + 1) * 128])
            for half in range(2):
                g = pair * 2 + half
                queries = stack_heads(q_ref[rows, g * 128:(g + 1) * 128])
                scores = dot(queries, keys[half], NT) * 0.125 + bias
                exponent = jnp.exp(scores - jnp.max(scores, axis=-1, keepdims=True))
                attention = (exponent / jnp.sum(exponent, axis=-1, keepdims=True)).astype(BF16)
                p_ref[pack, g] = attention
                att_ref[rows, g * 128:(g + 1) * 128] = join_heads(dot(attention, values[half], NN)).astype(BF16)

    arrive(copies, 3)
    for i in range(4):
        cols = slice(i * 256, (i + 1) * 256)
        middle_ref[:, cols] = hidden_ref[:, cols].astype(F32) + dot(att_ref[...], wo[:, cols], NN)
    middle = middle_ref[...]
    ne_ref[...] = (middle * scale_of(middle) * small[1:2].astype(F32)).astype(BF16)
    logits = dot(ne_ref[...], small, NT)
    marks = marks_ref[...] > 0.0
    peak = jnp.max(jnp.where(marks, logits, -1e30), axis=-1, keepdims=True)
    lifted = jnp.where(marks, jnp.exp(jnp.where(marks, logits - peak, 0.0)), 0.0)
    gates = lifted / jnp.sum(lifted, axis=-1, keepdims=True)
    gates_ref[...] = gates

    arrive(copies, 4, 5)
    for e in range(3):
        for i in range(2):
            cols = slice(i * 256, (i + 1) * 256)
            flat = slice(e * 512 + i * 256, e * 512 + (i + 1) * 256)
            gl = dot(ne_ref[...], wg[e, :, cols], NN)
            ul = dot(ne_ref[...], wu[e, :, cols], NN)
            gl_ref[:, flat] = gl.astype(BF16)
            ul_ref[:, flat] = ul.astype(BF16)
            inner = gl * jax.nn.sigmoid(gl) * ul
            gi_ref[:, flat] = (gates[:, 2 + e:3 + e] * inner).astype(BF16)

    arrive(copies, 6)
    for i in range(4):
        cols = slice(i * 256, (i + 1) * 256)
        total = middle_ref[:, cols]
        for e in range(3):
            total = total + dot(gi_ref[:, e * 512:(e + 1) * 512], wd[e, :, cols], NN)
        out_ref[:, cols] = total
        relay_ref[:, cols] = total.astype(BF16)


KEPT = (
    ((TOKENS, WIDTH), F32), ((TOKENS, WIDTH), BF16), ((TOKENS, WIDTH), BF16), ((TOKENS, WIDTH), BF16),
    ((TOKENS, 512), BF16), ((TOKENS, 512), BF16), ((2, 8, 256, 128), BF16), ((TOKENS, WIDTH), BF16),
    ((TOKENS, WIDTH), F32), ((TOKENS, WIDTH), BF16), ((TOKENS, 16), F32), ((TOKENS, 1536), BF16),
    ((TOKENS, 1536), BF16), ((TOKENS, 1536), BF16),
)


def specs(places):
    return [pl.BlockSpec(memory_space=place) for place in places]


def forward(start, received, bias, marks, cos, sin, small, weights, keep):
    scratch = [pltpu.VMEM(shape, BF16) for shape in WEIGHT_SHAPES] + [pltpu.SemaphoreType.DMA((14,))]
    outs = (((TOKENS, WIDTH), BF16),)
    if keep:
        outs = outs + KEPT
    else:
        scratch = [pltpu.VMEM(shape, kind) for shape, kind in KEPT] + scratch
    return pl.pallas_call(
        forward_kernel,
        out_shape=tuple(jax.ShapeDtypeStruct(shape, kind) for shape, kind in outs),
        in_specs=specs([pltpu.VMEM] * 8 + [pl.ANY] * 14),
        out_specs=tuple(specs([pltpu.VMEM] * len(outs))),
        scratch_shapes=scratch,
        compiler_params=pltpu.CompilerParams(vmem_limit_bytes=VMEM_LIMIT),
    )(start, received, bias, marks, cos, sin, *small, *weights[0], *weights[1])


def norm_back(rows, scale, gain, incoming):
    weighted = incoming * gain
    gain_part = jnp.sum(incoming * rows * scale, axis=0, keepdims=True)
    part = scale * weighted - rows * (scale * scale * scale) * jnp.mean(weighted * rows, axis=-1, keepdims=True)
    return part, gain_part


def backward_kernel(
    returned_ref, cotangent_ref, cos_ref, sin_ref, small_mine, small_other,
    hidden_ref, normed_ref, q_ref, k_ref, v_ref, p_ref, att_ref, middle_ref, ne_ref, gates_ref, gl_ref, ul_ref,
    *refs,
):
    mine, others, refs = refs[:7], refs[7:14], refs[14:]
    relay_ref, grad_ref, small_grad, up_ref, bgu_ref, bb_ref, bqkv_ref = refs[:7]
    held, (sems, bne_ref, bm_ref, ba_ref) = refs[7:14], refs[14:]
    wq, wk, wv, wo, wg, wu, wd = held
    copies = weight_copies(mine, others, held, sems)
    start_all(copies, (6, 4, 5, 3, 0, 1, 2))
    small = small_rows(small_mine, small_other)
    first = lax.axis_index("section") == 0
    up_ref[...] = jnp.where(first, returned_ref[...], cotangent_ref[...])
    gates = gates_ref[...]
    lane = lax.broadcasted_iota(jnp.int32, gates.shape, 1)
    pulls = jnp.zeros_like(gates)

    arrive(copies, 6)
    for e in range(3):
        gate = gates[:, 2 + e:3 + e]
        for i in range(2):
            flat = slice(e * 512 + i * 256, e * 512 + (i + 1) * 256)
            u = dot(up_ref[...], wd[e, i * 256:(i + 1) * 256, :], NT)
            gl = gl_ref[:, flat].astype(F32)
            ul = ul_ref[:, flat].astype(F32)
            sg = jax.nn.sigmoid(gl)
            silu = gl * sg
            pulls = pulls + jnp.where(lane == 2 + e, jnp.sum(u * silu * ul, axis=-1, keepdims=True), 0.0)
            inner = gate * u
            at = e * 1024 + i * 256
            bgu_ref[:, at:at + 256] = (inner * ul * sg * (1.0 + gl * (1.0 - sg))).astype(BF16)
            bgu_ref[:, at + 512:at + 768] = (inner * silu).astype(BF16)
    back_logits = (gates * (pulls - jnp.sum(gates * pulls, axis=-1, keepdims=True))).astype(BF16)

    arrive(copies, 4, 5)
    for i in range(4):
        cols = slice(i * 256, (i + 1) * 256)
        total = dot(back_logits, small[:, cols], NN)
        for e in range(3):
            total = total + dot(bgu_ref[:, e * 1024:e * 1024 + 512], wg[e, cols, :], NT)
            total = total + dot(bgu_ref[:, e * 1024 + 512:e * 1024 + 1024], wu[e, cols, :], NT)
        bne_ref[:, cols] = total
    middle = middle_ref[...]
    part, expert_gain = norm_back(middle, scale_of(middle), small[1:2].astype(F32), bne_ref[...])
    bm_ref[...] = up_ref[...].astype(F32) + part
    bb_ref[...] = bm_ref[...].astype(BF16)

    arrive(copies, 3)
    for i in range(4):
        cols = slice(i * 256, (i + 1) * 256)
        ba_ref[:, cols] = dot(bb_ref[...], wo[cols, :], NT).astype(BF16)

    cos, sin = cos_ref[0:128, 0:128], sin_ref[0:128, 0:128]

    def unturn(u):
        return (u * cos - swap_halves(u) * sin).astype(BF16)

    for pack in range(2):
        rows = slice(pack * 128, pack * 128 + 128)
        for pair in range(4):
            keys = both_ways(k_ref[rows, pair * 128:(pair + 1) * 128])
            values = both_ways(v_ref[rows, pair * 128:(pair + 1) * 128])
            back_k, back_v = [], []
            for half in range(2):
                g = pair * 2 + half
                cols = slice(g * 128, (g + 1) * 128)
                queries = stack_heads(q_ref[rows, cols])
                back_out = stack_heads(ba_ref[rows, cols])
                attention = p_ref[pack, g]
                wide = attention.astype(F32)
                pull = dot(back_out, values[half], NT)
                bv = dot(attention, back_out, TN)
                back_v.append(bv + pltpu.roll(bv, 64, 1))
                spread = wide * pull
                back_scores = (
                    (spread - wide * jnp.sum(spread, axis=-1, keepdims=True)) * 0.125
                ).astype(BF16)
                bqkv_ref[rows, cols] = unturn(join_heads(dot(back_scores, keys[half], NN)))
                bk = dot(back_scores, queries, TN)
                back_k.append(bk + pltpu.roll(bk, 64, 1))
            low = low_half((128, 128))
            at = 1024 + pair * 128
            bqkv_ref[rows, at:at + 128] = unturn(jnp.where(low, back_k[0], back_k[1]))
            bqkv_ref[rows, at + 512:at + 640] = jnp.where(low, back_v[0], back_v[1]).astype(BF16)

    arrive(copies, 0, 1, 2)
    for i in range(4):
        cols = slice(i * 256, (i + 1) * 256)
        total = dot(bqkv_ref[:, 0:1024], wq[cols, :], NT)
        total = total + dot(bqkv_ref[:, 1024:1536], wk[cols, :], NT)
        bne_ref[:, cols] = total + dot(bqkv_ref[:, 1536:2048], wv[cols, :], NT)
    x = hidden_ref[...].astype(F32)
    part, mixer_gain = norm_back(x, scale_of(x), small[0:1].astype(F32), bne_ref[...])
    total = bm_ref[...] + part
    grad_ref[...] = total
    relay_ref[...] = total.astype(BF16)

    router = dot(back_logits, ne_ref[...], TN)
    row = lax.broadcasted_iota(jnp.int32, router.shape, 0)
    mixed = jnp.where(row == 0, mixer_gain, jnp.where(row == 1, expert_gain, router))
    small_grad[0] = mixed[:, 0:512]
    small_grad[1] = mixed[:, 512:1024]


def backward(returned, cotangent, cos, sin, small, kept, weights, keep):
    hidden, normed, q, k, v, p, att, middle, ne, gates, gl, ul, gi = kept
    rest = (
        ((TOKENS, WIDTH), F32), ((2, 16, 512), F32), ((TOKENS, WIDTH), BF16), ((TOKENS, 3072), BF16),
        ((TOKENS, WIDTH), BF16), ((TOKENS, 2048), BF16),
    )
    outs = (((TOKENS, WIDTH), BF16),)
    scratch = [pltpu.VMEM(shape, BF16) for shape in WEIGHT_SHAPES] + [
        pltpu.SemaphoreType.DMA((14,)),
        pltpu.VMEM((TOKENS, WIDTH), F32), pltpu.VMEM((TOKENS, WIDTH), F32), pltpu.VMEM((TOKENS, WIDTH), BF16),
    ]
    if keep:
        outs = outs + rest
    else:
        scratch = [pltpu.VMEM(shape, kind) for shape, kind in rest] + scratch
    return pl.pallas_call(
        backward_kernel,
        out_shape=tuple(jax.ShapeDtypeStruct(shape, kind) for shape, kind in outs),
        in_specs=specs([pltpu.VMEM] * 18 + [pl.ANY] * 14),
        out_specs=tuple(specs([pltpu.VMEM] * len(outs))),
        scratch_shapes=scratch,
        compiler_params=pltpu.CompilerParams(vmem_limit_bytes=VMEM_LIMIT),
    )(returned, cotangent, cos, sin, *small, hidden, normed, q, k, v, p, att, middle, ne, gates, gl, ul,
      *weights[0], *weights[1])


def weight_grad_kernel(normed_ref, att_ref, ne_ref, gi_ref, up_ref, bgu_ref, bb_ref, bqkv_ref, out_ref, held, sems):
    copies = []

    def tile(a, a_at, count, b, b_at, half, at):
        value = dot(a[:, a_at:a_at + count], b[:, b_at:b_at + 512], TN)
        held[half, at:at + count, :] = value.astype(BF16)

    def send(half, at, count):
        place = (half, pl.ds(at, count))
        copy = pltpu.make_async_copy(held.at[place], out_ref.at[place], sems.at[len(copies)])
        copy.start()
        copies.append(copy)

    for half in range(2):
        for i in range(2):
            tile(normed_ref, half * 512, 512, bqkv_ref, i * 512, half, i * 512)
            tile(normed_ref, half * 512, 512, bqkv_ref, 1024 + i * 512, half, 1024 + i * 512)
            tile(att_ref, half * 512, 512, bb_ref, i * 512, half, 2048 + i * 512)
        send(half, 0, 3072)
        for e in range(3):
            for i in range(2):
                tile(ne_ref, half * 512, 512, bgu_ref, e * 1024 + i * 512, half, 3072 + e * 1024 + i * 512)
        send(half, 3072, 3072)
        for e in range(3):
            for i in range(2):
                tile(gi_ref, e * 512 + half * 256, 256, up_ref, i * 512, half, 6144 + e * 512 + i * 256)
        send(half, 6144, 1536)
    for copy in copies:
        copy.wait()


def weight_grads(normed, att, ne, gi, up, bgu, bb, bqkv):
    return pl.pallas_call(
        weight_grad_kernel,
        out_shape=jax.ShapeDtypeStruct((2, ROWS, COLS), BF16),
        in_specs=specs([pltpu.VMEM] * 8),
        out_specs=pl.BlockSpec(memory_space=pl.ANY),
        scratch_shapes=[pltpu.VMEM((2, ROWS, COLS), BF16), pltpu.SemaphoreType.DMA((6,))],
        compiler_params=pltpu.CompilerParams(vmem_limit_bytes=VMEM_LIMIT),
    )(normed, att, ne, gi, up, bgu, bb, bqkv)


def rotary_tables():
    lane = np.arange(256)
    frequency = np.power(10000.0, -2.0 * (lane % 32) / 64.0)
    angles = (np.arange(TOKENS) % 128)[:, None] * frequency[None, :]
    sign = np.where(lane % 64 < 32, -1.0, 1.0)[None, :]
    return np.cos(angles).astype(np.float32), (np.sin(angles) * sign).astype(np.float32)


def body(
    inputs, cotangent, segments, routes, mixer_gain, query_weight, key_matrix, value_matrix, out_weight,
    expert_gain, router_weight, gate_weight, up_weight, down_weight,
):
    start = inputs.reshape(TOKENS, WIDTH)
    loss = cotangent.reshape(TOKENS, WIDTH)
    small_mine = jnp.concatenate(
        [mixer_gain, expert_gain, jnp.transpose(router_weight[0]), jnp.zeros((11, 512), BF16)], axis=0
    )
    mine = (
        query_weight[0], key_matrix[0], value_matrix[0], out_weight[0], gate_weight[0], up_weight[0],
        down_weight[0],
    )
    *others, small_other = exchange(*mine, small_mine)
    weights = (mine, tuple(others))
    small = (small_mine, small_other)
    seg = segments[:, 0]
    place = jnp.arange(128, dtype=jnp.int32)
    allowed = (seg[:, :, None] == seg[:, None, :]) & (place[None, None, :] <= place[None, :, None])
    bias = jnp.where(allowed, 0.0, -1e30).astype(F32)
    picks = routes.reshape(TOKENS, 2)
    columns = jnp.arange(16, dtype=jnp.int32)[None, :] - 2
    marks = ((picks[:, 0:1] == columns) | (picks[:, 1:2] == columns)).astype(F32)
    cos, sin = (jnp.asarray(table) for table in rotary_tables())

    (relay,) = forward(start, start, bias, marks, cos, sin, small, weights, False)
    received = lax.ppermute(relay, "section", [(0, 1)])
    relay, out, *kept = forward(start, received, bias, marks, cos, sin, small, weights, True)
    (relay,) = backward(loss, loss, cos, sin, small, kept, weights, False)
    returned = lax.ppermute(relay, "section", [(1, 0)])
    relay, grad, small_grad, up, bgu, bb, bqkv = backward(
        returned, loss, cos, sin, small, kept, weights, True
    )
    parts = weight_grads(kept[1], kept[6], kept[8], kept[12], up, bgu, bb, bqkv)
    total, small_total = reduce_gradients(parts, small_grad)

    def wide(at, rows):
        return jnp.concatenate([total[at:at + rows], total[at + rows:at + 2 * rows]], axis=1).astype(F32)

    experts = total[3072:6144].reshape(3, 2, 512, 512).astype(F32)
    down = total[6144:7680].reshape(3, 2, 256, 512)
    down = jnp.concatenate([down[:, 0], down[:, 1]], axis=-1).astype(F32)
    return (
        out.reshape(1, 2, 1, 128, WIDTH),
        grad.reshape(1, 2, 1, 128, WIDTH),
        small_total[0:1],
        wide(0, 512)[None],
        total[1024:1536].astype(F32)[None],
        total[1536:2048].astype(F32)[None],
        wide(2048, 512)[None],
        small_total[1:2],
        jnp.transpose(small_total[2:5])[None],
        experts[:, 0][None],
        experts[:, 1][None],
        down[None],
    )


def solution(mesh):
    return jax.shard_map(
        body,
        mesh=mesh,
        in_specs=(
            P(None, ("shard", "replica"), None, None),
            P(None, ("shard", "replica"), None, None),
            P(None, ("shard", "replica"), None),
            P("section", None, ("shard", "replica"), None, None),
            P("section", "shard"),
            P("section", "shard", None),
            P("section", "shard", None),
            P("section", "shard", None),
            P("section", "shard", None),
            P("section", "shard"),
            P("section", "shard", None),
            P("section", None, "shard", None),
            P("section", None, "shard", None),
            P("section", None, "shard", None),
        ),
        out_specs=(
            P("section", None, ("shard", "replica"), None, None),
            P("section", None, ("shard", "replica"), None, None),
            P("section", "shard"),
            P("section", "shard", None),
            P("section", "shard", None),
            P("section", "shard", None),
            P("section", "shard", None),
            P("section", "shard"),
            P("section", "shard", None),
            P("section", None, "shard", None),
            P("section", None, "shard", None),
            P("section", None, "shard", None),
        ),
        check_vma=False,
    )
```

```python
import functools

import numpy as np
import jax
import jax.numpy as jnp
from jax import lax
from jax.experimental import pallas as pl
from jax.experimental.pallas import tpu as pltpu
from jax.sharding import PartitionSpec as P

MESH = pl.DeviceIdType.MESH
ROWS = 7680
COLS = 512
PARTS = 5
PART = ROWS // PARTS
DIMS = 5


def gather_kernel(count, *refs):
    mine, others = refs[:count], refs[count:2 * count]
    send_sem, recv_sem = refs[2 * count:]
    sibling = {"shard": 1 - lax.axis_index("shard")}
    barrier = pltpu.get_barrier_semaphore()
    pl.semaphore_signal(barrier, inc=1, device_id=sibling, device_id_type=MESH)
    pl.semaphore_wait(barrier, 1)
    copies = []
    for i in range(count):
        copy = pltpu.make_async_remote_copy(
            src_ref=mine[i], dst_ref=others[i],
            send_sem=send_sem.at[i], recv_sem=recv_sem.at[i],
            device_id=sibling, device_id_type=MESH,
        )
        copy.start()
        copies.append(copy)
    for copy in copies:
        copy.wait()


def exchange(*arrays):
    n = len(arrays)
    return pl.pallas_call(
        functools.partial(gather_kernel, n),
        out_shape=tuple(jax.ShapeDtypeStruct(a.shape, a.dtype) for a in arrays),
        in_specs=[pl.BlockSpec(memory_space=pl.ANY)] * n,
        out_specs=tuple(pl.BlockSpec(memory_space=pl.ANY) for _ in arrays),
        scratch_shapes=[pltpu.SemaphoreType.DMA((n,)), pltpu.SemaphoreType.DMA((n,))],
        compiler_params=pltpu.CompilerParams(collective_id=2, has_side_effects=True),
    )(*arrays)


EPSILON = 1e-06
WEIGHT_SHAPES = (
    (1024, 1024), (1024, 512), (1024, 512), (1024, 1024), (3, 1024, 512), (3, 1024, 512), (3, 512, 1024),
)
NT = (((1,), (1,)), ((), ()))
NN = (((1,), (0,)), ((), ()))
TN = (((0,), (0,)), ((), ()))
F32 = jnp.float32
BF16 = jnp.bfloat16
TOKENS = 256
WIDTH = 1024
VMEM_LIMIT = 56 * 1024 * 1024


def dot(a, b, dims):
    return lax.dot_general(a, b, dims, preferred_element_type=F32)


def weight_copies(mine, others, held, sems):
    core = lax.axis_index("shard")
    copies = []
    for i, (a, b, w) in enumerate(zip(mine, others, held)):
        rows = a.shape[-2]
        axis = len(a.shape) - 2
        pair = []
        for j, (source, owner) in enumerate(((a, core), (b, 1 - core))):
            place = pl.ds(pl.multiple_of(owner * rows, rows), rows)
            target = w.at[place] if axis == 0 else w.at[:, place]
            pair.append(pltpu.make_async_copy(source, target, sems.at[2 * i + j]))
        copies.append(pair)
    return copies


def start_all(copies, order):
    for i in order:
        for copy in copies[i]:
            copy.start()


def arrive(copies, *which):
    for i in which:
        for copy in copies[i]:
            copy.wait()


def small_rows(mine, other):
    first = lax.axis_index("shard") == 0
    a, b = mine[...], other[...]
    return jnp.concatenate([jnp.where(first, a, b), jnp.where(first, b, a)], axis=1)


def scale_of(rows):
    return lax.rsqrt(jnp.mean(rows * rows, axis=-1, keepdims=True) + EPSILON)


def swap_halves(u):
    lanes = u.shape[1]
    lane = lax.broadcasted_iota(jnp.int32, u.shape, 1)
    return jnp.where(lane % 64 < 32, pltpu.roll(u, lanes - 32, 1), pltpu.roll(u, 32, 1))


def low_half(shape):
    return lax.broadcasted_iota(jnp.int32, shape, 1) < 64


def both_ways(block):
    wide = block.astype(F32)
    turned = pltpu.roll(wide, 64, 1)
    low = low_half(wide.shape)
    return jnp.where(low, wide, turned).astype(BF16), jnp.where(low, turned, wide).astype(BF16)


def stack_heads(block):
    wide = block.astype(F32)
    low = low_half(wide.shape)
    zero = jnp.zeros_like(wide)
    return jnp.concatenate([jnp.where(low, wide, zero), jnp.where(low, zero, wide)], axis=0).astype(BF16)


def join_heads(rows):
    return jnp.where(low_half((128, 128)), rows[:128], rows[128:])


def forward_kernel(
    start_ref, received_ref, bias_ref, marks_ref, cos_ref, sin_ref, small_mine, small_other, *refs
):
    mine, others, refs = refs[:7], refs[7:14], refs[14:]
    (relay_ref, out_ref, hidden_ref, normed_ref, q_ref, k_ref, v_ref, p_ref, att_ref, middle_ref, ne_ref,
     gates_ref, gl_ref, ul_ref, gi_ref) = refs[:15]
    held, sems = refs[15:22], refs[22]
    wq, wk, wv, wo, wg, wu, wd = held
    copies = weight_copies(mine, others, held, sems)
    start_all(copies, range(7))
    small = small_rows(small_mine, small_other)
    first = lax.axis_index("section") == 0
    hidden = jnp.where(first, start_ref[...], received_ref[...])
    hidden_ref[...] = hidden
    x = hidden.astype(F32)
    normed_ref[...] = (x * scale_of(x) * small[0:1].astype(F32)).astype(BF16)

    def block(ref, i, size=256):
        return ref[:, i * size:(i + 1) * size]

    for weight, target, number, turned, index in (
        (wq, q_ref, 4, True, 0), (wk, k_ref, 2, True, 1), (wv, v_ref, 2, False, 2),
    ):
        arrive(copies, index)
        for i in range(number):
            u = dot(normed_ref[...], block(weight, i), NN)
            if turned:
                u = u * cos_ref[...] + swap_halves(u) * sin_ref[...]
            target[:, i * 256:(i + 1) * 256] = u.astype(BF16)

    for pack in range(2):
        rows = slice(pack * 128, pack * 128 + 128)
        bias = bias_ref[pack]
        bias = jnp.concatenate([bias, bias], axis=0)
        for pair in range(4):
            keys = both_ways(k_ref[rows, pair * 128:(pair + 1) * 128])
            values = both_ways(v_ref[rows, pair * 128:(pair + 1) * 128])
            for half in range(2):
                g = pair * 2 + half
                queries = stack_heads(q_ref[rows, g * 128:(g + 1) * 128])
                scores = dot(queries, keys[half], NT) * 0.125 + bias
                exponent = jnp.exp(scores - jnp.max(scores, axis=-1, keepdims=True))
                attention = (exponent / jnp.sum(exponent, axis=-1, keepdims=True)).astype(BF16)
                p_ref[pack, g] = attention
                att_ref[rows, g * 128:(g + 1) * 128] = join_heads(dot(attention, values[half], NN)).astype(BF16)

    arrive(copies, 3)
    for i in range(4):
        cols = slice(i * 256, (i + 1) * 256)
        middle_ref[:, cols] = hidden_ref[:, cols].astype(F32) + dot(att_ref[...], wo[:, cols], NN)
    middle = middle_ref[...]
    ne_ref[...] = (middle * scale_of(middle) * small[1:2].astype(F32)).astype(BF16)
    logits = dot(ne_ref[...], small, NT)
    marks = marks_ref[...] > 0.0
    peak = jnp.max(jnp.where(marks, logits, -1e30), axis=-1, keepdims=True)
    lifted = jnp.where(marks, jnp.exp(jnp.where(marks, logits - peak, 0.0)), 0.0)
    gates = lifted / jnp.sum(lifted, axis=-1, keepdims=True)
    gates_ref[...] = gates

    arrive(copies, 4, 5)
    for e in range(3):
        for i in range(2):
            cols = slice(i * 256, (i + 1) * 256)
            flat = slice(e * 512 + i * 256, e * 512 + (i + 1) * 256)
            gl = dot(ne_ref[...], wg[e, :, cols], NN)
            ul = dot(ne_ref[...], wu[e, :, cols], NN)
            gl_ref[:, flat] = gl.astype(BF16)
            ul_ref[:, flat] = ul.astype(BF16)
            inner = gl * jax.nn.sigmoid(gl) * ul
            gi_ref[:, flat] = (gates[:, 2 + e:3 + e] * inner).astype(BF16)

    arrive(copies, 6)
    for i in range(4):
        cols = slice(i * 256, (i + 1) * 256)
        total = middle_ref[:, cols]
        for e in range(3):
            total = total + dot(gi_ref[:, e * 512:(e + 1) * 512], wd[e, :, cols], NN)
        out_ref[:, cols] = total
        relay_ref[:, cols] = total.astype(BF16)


KEPT = (
    ((TOKENS, WIDTH), F32), ((TOKENS, WIDTH), BF16), ((TOKENS, WIDTH), BF16), ((TOKENS, WIDTH), BF16),
    ((TOKENS, 512), BF16), ((TOKENS, 512), BF16), ((2, 8, 256, 128), BF16), ((TOKENS, WIDTH), BF16),
    ((TOKENS, WIDTH), F32), ((TOKENS, WIDTH), BF16), ((TOKENS, 16), F32), ((TOKENS, 1536), BF16),
    ((TOKENS, 1536), BF16), ((TOKENS, 1536), BF16),
)


def specs(places):
    return [pl.BlockSpec(memory_space=place) for place in places]


def forward(start, received, bias, marks, cos, sin, small, weights, keep):
    scratch = [pltpu.VMEM(shape, BF16) for shape in WEIGHT_SHAPES] + [pltpu.SemaphoreType.DMA((14,))]
    outs = (((TOKENS, WIDTH), BF16),)
    if keep:
        outs = outs + KEPT
    else:
        scratch = [pltpu.VMEM(shape, kind) for shape, kind in KEPT] + scratch
    return pl.pallas_call(
        forward_kernel,
        out_shape=tuple(jax.ShapeDtypeStruct(shape, kind) for shape, kind in outs),
        in_specs=specs([pltpu.VMEM] * 8 + [pl.ANY] * 14),
        out_specs=tuple(specs([pltpu.VMEM] * len(outs))),
        scratch_shapes=scratch,
        compiler_params=pltpu.CompilerParams(vmem_limit_bytes=VMEM_LIMIT),
    )(start, received, bias, marks, cos, sin, *small, *weights[0], *weights[1])


def norm_back(rows, scale, gain, incoming):
    weighted = incoming * gain
    gain_part = jnp.sum(incoming * rows * scale, axis=0, keepdims=True)
    part = scale * weighted - rows * (scale * scale * scale) * jnp.mean(weighted * rows, axis=-1, keepdims=True)
    return part, gain_part


def backward_kernel(
    returned_ref, cotangent_ref, cos_ref, sin_ref, small_mine, small_other,
    hidden_ref, normed_ref, q_ref, k_ref, v_ref, p_ref, att_ref, middle_ref, ne_ref, gates_ref, gl_ref, ul_ref,
    *refs,
):
    mine, others, refs = refs[:7], refs[7:14], refs[14:]
    relay_ref, grad_ref, small_grad, up_ref, bgu_ref, bb_ref, bqkv_ref = refs[:7]
    held, (sems, bne_ref, bm_ref, ba_ref) = refs[7:14], refs[14:]
    wq, wk, wv, wo, wg, wu, wd = held
    copies = weight_copies(mine, others, held, sems)
    start_all(copies, (6, 4, 5, 3, 0, 1, 2))
    small = small_rows(small_mine, small_other)
    first = lax.axis_index("section") == 0
    up_ref[...] = jnp.where(first, returned_ref[...], cotangent_ref[...])
    gates = gates_ref[...]
    lane = lax.broadcasted_iota(jnp.int32, gates.shape, 1)
    pulls = jnp.zeros_like(gates)

    arrive(copies, 6)
    for e in range(3):
        gate = gates[:, 2 + e:3 + e]
        for i in range(2):
            flat = slice(e * 512 + i * 256, e * 512 + (i + 1) * 256)
            u = dot(up_ref[...], wd[e, i * 256:(i + 1) * 256, :], NT)
            gl = gl_ref[:, flat].astype(F32)
            ul = ul_ref[:, flat].astype(F32)
            sg = jax.nn.sigmoid(gl)
            silu = gl * sg
            pulls = pulls + jnp.where(lane == 2 + e, jnp.sum(u * silu * ul, axis=-1, keepdims=True), 0.0)
            inner = gate * u
            at = e * 1024 + i * 256
            bgu_ref[:, at:at + 256] = (inner * ul * sg * (1.0 + gl * (1.0 - sg))).astype(BF16)
            bgu_ref[:, at + 512:at + 768] = (inner * silu).astype(BF16)
    back_logits = (gates * (pulls - jnp.sum(gates * pulls, axis=-1, keepdims=True))).astype(BF16)

    arrive(copies, 4, 5)
    for i in range(4):
        cols = slice(i * 256, (i + 1) * 256)
        total = dot(back_logits, small[:, cols], NN)
        for e in range(3):
            total = total + dot(bgu_ref[:, e * 1024:e * 1024 + 512], wg[e, cols, :], NT)
            total = total + dot(bgu_ref[:, e * 1024 + 512:e * 1024 + 1024], wu[e, cols, :], NT)
        bne_ref[:, cols] = total
    middle = middle_ref[...]
    part, expert_gain = norm_back(middle, scale_of(middle), small[1:2].astype(F32), bne_ref[...])
    bm_ref[...] = up_ref[...].astype(F32) + part
    bb_ref[...] = bm_ref[...].astype(BF16)

    arrive(copies, 3)
    for i in range(4):
        cols = slice(i * 256, (i + 1) * 256)
        ba_ref[:, cols] = dot(bb_ref[...], wo[cols, :], NT).astype(BF16)

    cos, sin = cos_ref[0:128, 0:128], sin_ref[0:128, 0:128]

    def unturn(u):
        return (u * cos - swap_halves(u) * sin).astype(BF16)

    for pack in range(2):
        rows = slice(pack * 128, pack * 128 + 128)
        for pair in range(4):
            keys = both_ways(k_ref[rows, pair * 128:(pair + 1) * 128])
            values = both_ways(v_ref[rows, pair * 128:(pair + 1) * 128])
            back_k, back_v = [], []
            for half in range(2):
                g = pair * 2 + half
                cols = slice(g * 128, (g + 1) * 128)
                queries = stack_heads(q_ref[rows, cols])
                back_out = stack_heads(ba_ref[rows, cols])
                attention = p_ref[pack, g]
                wide = attention.astype(F32)
                pull = dot(back_out, values[half], NT)
                bv = dot(attention, back_out, TN)
                back_v.append(bv + pltpu.roll(bv, 64, 1))
                spread = wide * pull
                back_scores = (
                    (spread - wide * jnp.sum(spread, axis=-1, keepdims=True)) * 0.125
                ).astype(BF16)
                bqkv_ref[rows, cols] = unturn(join_heads(dot(back_scores, keys[half], NN)))
                bk = dot(back_scores, queries, TN)
                back_k.append(bk + pltpu.roll(bk, 64, 1))
            low = low_half((128, 128))
            at = 1024 + pair * 128
            bqkv_ref[rows, at:at + 128] = unturn(jnp.where(low, back_k[0], back_k[1]))
            bqkv_ref[rows, at + 512:at + 640] = jnp.where(low, back_v[0], back_v[1]).astype(BF16)

    arrive(copies, 0, 1, 2)
    for i in range(4):
        cols = slice(i * 256, (i + 1) * 256)
        total = dot(bqkv_ref[:, 0:1024], wq[cols, :], NT)
        total = total + dot(bqkv_ref[:, 1024:1536], wk[cols, :], NT)
        bne_ref[:, cols] = total + dot(bqkv_ref[:, 1536:2048], wv[cols, :], NT)
    x = hidden_ref[...].astype(F32)
    part, mixer_gain = norm_back(x, scale_of(x), small[0:1].astype(F32), bne_ref[...])
    total = bm_ref[...] + part
    grad_ref[...] = total
    relay_ref[...] = total.astype(BF16)

    router = dot(back_logits, ne_ref[...], TN)
    row = lax.broadcasted_iota(jnp.int32, router.shape, 0)
    mixed = jnp.where(row == 0, mixer_gain, jnp.where(row == 1, expert_gain, router))
    small_grad[0] = mixed[:, 0:512]
    small_grad[1] = mixed[:, 512:1024]


def backward(returned, cotangent, cos, sin, small, kept, weights, keep):
    hidden, normed, q, k, v, p, att, middle, ne, gates, gl, ul, gi = kept
    rest = (
        ((TOKENS, WIDTH), F32), ((2, 16, 512), F32), ((TOKENS, WIDTH), BF16), ((TOKENS, 3072), BF16),
        ((TOKENS, WIDTH), BF16), ((TOKENS, 2048), BF16),
    )
    outs = (((TOKENS, WIDTH), BF16),)
    scratch = [pltpu.VMEM(shape, BF16) for shape in WEIGHT_SHAPES] + [
        pltpu.SemaphoreType.DMA((14,)),
        pltpu.VMEM((TOKENS, WIDTH), F32), pltpu.VMEM((TOKENS, WIDTH), F32), pltpu.VMEM((TOKENS, WIDTH), BF16),
    ]
    if keep:
        outs = outs + rest
    else:
        scratch = [pltpu.VMEM(shape, kind) for shape, kind in rest] + scratch
    return pl.pallas_call(
        backward_kernel,
        out_shape=tuple(jax.ShapeDtypeStruct(shape, kind) for shape, kind in outs),
        in_specs=specs([pltpu.VMEM] * 18 + [pl.ANY] * 14),
        out_specs=tuple(specs([pltpu.VMEM] * len(outs))),
        scratch_shapes=scratch,
        compiler_params=pltpu.CompilerParams(vmem_limit_bytes=VMEM_LIMIT),
    )(returned, cotangent, cos, sin, *small, hidden, normed, q, k, v, p, att, middle, ne, gates, gl, ul,
      *weights[0], *weights[1])


def cube_position():
    r = lax.axis_index("replica")
    x = r % 4
    z = (r // 4) % 4
    y = r // 16
    bits = (((x + 1) // 2) % 2, x // 2, ((z + 1) // 2) % 2, z // 2, y)
    partners = (
        r + 1 - 2 * (x % 2),
        r + 3 - 2 * x,
        r + 4 - 8 * (z % 2),
        r + 12 - 8 * z,
        (r + 16) % 32,
    )
    return bits, partners


def rows_at(at, count):
    if isinstance(at, int):
        return pl.ds(at, count)
    return pl.ds(pl.multiple_of(at, 16), count)


def add_rows(dst, dst_at, a, a_at, b, b_at, count):
    step = min(count, 192)

    def one(i, carry):
        at = i * step
        dst[rows_at(dst_at + at, step), :] = (
            a[rows_at(a_at + at, step), :] + b[rows_at(b_at + at, step), :]
        )
        return carry

    lax.fori_loop(0, count // step, one, 0)


def reduce_kernel(
    normed_ref, att_ref, ne_ref, gi_ref, up_ref, bgu_ref, bb_ref, bqkv_ref, small_ref,
    out_ref, small_out,
    work, lent, from_core, from_cube, whole, small_held, small_got,
    core_send, core_recv, cube_send, cube_recv, share_send, share_recv, small_send, small_recv, store_sem,
):
    core = lax.axis_index("shard")
    bits, partners = cube_position()
    sibling = {"shard": 1 - core}

    barrier = pltpu.get_barrier_semaphore()
    pl.semaphore_signal(barrier, inc=1, device_id=sibling, device_id_type=MESH)
    for partner in partners:
        pl.semaphore_signal(barrier, inc=1, device_id={"replica": partner}, device_id_type=MESH)

    def tiles(p, target, half):
        def tile(a, a_at, count, b, b_at, at):
            rows = a[:, pl.ds(pl.multiple_of(a_at, 256), count)]
            target[at:at + count, :] = dot(rows, b[:, b_at:b_at + 512], TN).astype(BF16)

        left = half * 512
        if p == 0:
            for i in range(2):
                tile(normed_ref, left, 512, bqkv_ref, i * 512, i * 512)
            tile(normed_ref, left, 512, bqkv_ref, 1024, 1024)
        elif p == 1:
            tile(normed_ref, left, 512, bqkv_ref, 1536, 1536)
            for i in range(2):
                tile(att_ref, left, 512, bb_ref, i * 512, 2048 + i * 512)
        elif p < 4:
            for i in range(3 * p - 6, 3 * p - 3):
                tile(ne_ref, left, 512, bgu_ref, i * 512, 3072 + i * 512)
        else:
            for e in range(3):
                for i in range(2):
                    tile(gi_ref, e * 512 + half * 256, 256, up_ref, i * 512, 6144 + e * 512 + i * 256)

    sends = []

    def remote(source, target, send_sem, recv_sem, device):
        copy = pltpu.make_async_remote_copy(
            src_ref=source, dst_ref=target, send_sem=send_sem, recv_sem=recv_sem,
            device_id=device, device_id_type=MESH,
        )
        copy.start()
        sends.append(copy)
        return copy

    size = [PART >> s for s in range(DIMS + 1)]
    bit = [[bits[(p + s) % DIMS] for s in range(DIMS)] for p in range(PARTS)]
    device = [[{"replica": partners[(p + s) % DIMS]} for s in range(DIMS)] for p in range(PARTS)]
    held = [[p * PART] for p in range(PARTS)]
    for p in range(PARTS):
        for s in range(DIMS):
            held[p].append(held[p][s] + bit[p][s] * size[s + 1])

    def away(p, s):
        return held[p][s] + (1 - bit[p][s]) * size[s + 1]

    def core_piece(p, piece):
        at = away(p, 0) if piece == 0 else held[p][1]
        rows = rows_at(at, size[1])
        return remote(
            lent.at[rows], from_core.at[rows], core_send.at[2 * p + piece], core_recv.at[2 * p + piece], sibling
        )

    def slot(p, s, piece):
        return p * PART + PART - size[s] + piece * size[s + 2]

    def scatter(p, s):
        copies = []
        for piece in range(2 if s < DIMS - 1 else 1):
            index = (p * DIMS + s) * 2 + piece
            if s < DIMS - 1:
                b = bit[p][s + 1]
                at = away(p, s) + ((1 - b) if piece == 0 else b) * size[s + 2]
                count = size[s + 2]
                into = slot(p, s, piece)
            else:
                at, count, into = away(p, s), size[s + 1], p * PART + PART - size[s]
            copies.append(remote(
                work.at[rows_at(at, count)], from_cube.at[rows_at(into, count)],
                cube_send.at[index], cube_recv.at[index], device[p][s],
            ))
        return copies

    def share(p, s, at, piece):
        count = size[s + 2] if s < DIMS - 1 else size[DIMS]
        index = (p * DIMS + s) * 2 + piece
        rows = rows_at(at, count)
        return remote(whole.at[rows], whole.at[rows], share_send.at[index], share_recv.at[index], device[p][s])

    stores = []

    def store(at, count):
        rows = rows_at(at, count)
        copy = pltpu.make_async_copy(whole.at[rows], out_ref.at[rows], store_sem.at[len(stores)])
        copy.start()
        stores.append(copy)

    pl.semaphore_wait(barrier, 1 + DIMS)
    small = remote(small_ref.at[1 - core], small_got.at[0], small_send.at[0], small_recv.at[0], sibling)
    first = [None] * PARTS
    cube = [None] * PARTS

    def begin(p):
        first[p].wait_recv()
        at = away(p, 0)
        add_rows(work, at, work, at, from_core, at, size[1])
        cube[p] = scatter(p, 0)

    for p in range(PARTS):
        tiles(p, lent, 1 - core)
        first[p] = core_piece(p, 0)
        tiles(p, work, core)
        if p > 0:
            begin(p - 1)
    second = [core_piece(p, 1) for p in range(PARTS)]
    begin(PARTS - 1)
    small.wait_recv()
    small_held[0] = small_ref[core] + small_got[0]
    small = remote(
        small_held.at[0], small_got.at[1], small_send.at[1], small_recv.at[1], {"replica": partners[0]}
    )
    for p in range(PARTS):
        second[p].wait_recv()
        at = held[p][1]
        add_rows(work, at, work, at, from_core, at, size[1])

    shared = [None] * PARTS
    for s in range(DIMS):
        later = [None] * PARTS
        for p in range(PARTS):
            copies = cube[p]
            copies[0].wait_recv()
            if s < DIMS - 1:
                at = away(p, s + 1)
                add_rows(work, at, work, at, from_cube, slot(p, s, 0), size[s + 2])
                later[p] = copies[1]
                cube[p] = scatter(p, s + 1)
            else:
                at = held[p][DIMS]
                add_rows(whole, at, work, at, from_cube, p * PART + PART - size[s], size[DIMS])
                shared[p] = {(s, 0): share(p, s, at, 0), (s - 1, 0): share(p, s - 1, at, 0)}
                store(at, size[DIMS])
        if s < DIMS - 1:
            for p in range(PARTS):
                later[p].wait_recv()
                at = held[p][s + 2]
                add_rows(work, at, work, at, from_cube, slot(p, s, 1), size[s + 2])
        small.wait_recv()
        if s < DIMS - 1:
            small_held[s + 1] = small_held[s] + small_got[s + 1]
            small = remote(
                small_held.at[s + 1], small_got.at[s + 2], small_send.at[s + 2], small_recv.at[s + 2],
                {"replica": partners[s + 1]},
            )
        else:
            small_out[...] = small_held[s] + small_got[s + 1]

    for s in reversed(range(DIMS)):
        for p in range(PARTS):
            shared[p][(s, 0)].wait_recv()
            if s < DIMS - 1:
                shared[p][(s, 1)].wait_recv()
            got = away(p, s)
            if s > 0:
                shared[p][(s - 1, 1)] = share(p, s - 1, got, 1)
            if s > 1:
                shared[p][(s - 2, 0)] = share(p, s - 2, held[p][s], 0)
            store(got, size[s + 1])

    for copy in sends:
        copy.wait_send()
    for copy in stores:
        copy.wait()


def reduce_gradients(pieces, small):
    dma = pltpu.SemaphoreType.DMA
    buffer = pltpu.VMEM((ROWS, COLS), BF16)
    return pl.pallas_call(
        reduce_kernel,
        out_shape=(
            jax.ShapeDtypeStruct((ROWS, COLS), BF16),
            jax.ShapeDtypeStruct((16, COLS), F32),
        ),
        in_specs=specs([pltpu.VMEM] * 9),
        out_specs=tuple(specs([pl.ANY, pltpu.VMEM])),
        scratch_shapes=[
            buffer, buffer, buffer, buffer, buffer,
            pltpu.VMEM((DIMS, 16, COLS), F32),
            pltpu.VMEM((DIMS + 1, 16, COLS), F32),
            dma((2 * PARTS,)), dma((2 * PARTS,)),
            dma((2 * PARTS * DIMS,)), dma((2 * PARTS * DIMS,)),
            dma((2 * PARTS * DIMS,)), dma((2 * PARTS * DIMS,)),
            dma((DIMS + 1,)), dma((DIMS + 1,)),
            dma((PARTS + PARTS * DIMS,)),
        ],
        compiler_params=pltpu.CompilerParams(
            collective_id=1, has_side_effects=True, vmem_limit_bytes=VMEM_LIMIT
        ),
    )(*pieces, small)


def unpack_kernel(
    total_ref, small_ref, mixer_ref, query_ref, key_ref, value_ref, out_ref, expert_ref, router_ref,
    gate_ref, up_ref, down_ref, got, wide, load_sem, store_sem,
):
    loads = []
    for i in range(15):
        rows = pl.ds(i * 512, 512)
        copy = pltpu.make_async_copy(total_ref.at[rows], got.at[rows], load_sem.at[i])
        copy.start()
        loads.append(copy)
    small = small_ref[...]
    mixer_ref[...] = small[0:1]
    expert_ref[...] = small[1:2]
    router_ref[...] = jnp.transpose(small)[:, 2:5]
    stores = []

    def put(at, count, target):
        wide[at:at + count, :] = got[at:at + count, :].astype(F32)
        copy = pltpu.make_async_copy(wide.at[pl.ds(at, count)], target, store_sem.at[len(stores)])
        copy.start()
        stores.append(copy)

    for i in range(15):
        loads[i].wait()
        at = i * 512
        cols = pl.ds((i % 2) * 512, 512)
        if i < 2:
            put(at, 512, query_ref.at[:, cols])
        elif i == 2:
            put(at, 512, key_ref)
        elif i == 3:
            put(at, 512, value_ref)
        elif i < 6:
            put(at, 512, out_ref.at[:, cols])
        elif i < 12:
            e, which = (i - 6) // 2, (i - 6) % 2
            put(at, 512, (up_ref if which else gate_ref).at[e])
        else:
            for j in range(2):
                put(at + j * 256, 256, down_ref.at[i - 12, :, pl.ds(j * 512, 512)])
    for copy in stores:
        copy.wait()


def unpack(total, small):
    shapes = (
        (1, 512), (512, 1024), (512, 512), (512, 512), (512, 1024), (1, 512), (512, 3),
        (3, 512, 512), (3, 512, 512), (3, 256, 1024),
    )
    places = [pl.ANY if i not in (0, 5, 6) else pltpu.VMEM for i in range(10)]
    return pl.pallas_call(
        unpack_kernel,
        out_shape=tuple(jax.ShapeDtypeStruct(shape, F32) for shape in shapes),
        in_specs=specs([pl.ANY, pltpu.VMEM]),
        out_specs=tuple(specs(places)),
        scratch_shapes=[
            pltpu.VMEM((ROWS, COLS), BF16), pltpu.VMEM((ROWS, COLS), F32),
            pltpu.SemaphoreType.DMA((15,)), pltpu.SemaphoreType.DMA((18,)),
        ],
        compiler_params=pltpu.CompilerParams(vmem_limit_bytes=VMEM_LIMIT),
    )(total, small)


def rotary_tables():
    lane = np.arange(256)
    frequency = np.power(10000.0, -2.0 * (lane % 32) / 64.0)
    angles = (np.arange(TOKENS) % 128)[:, None] * frequency[None, :]
    sign = np.where(lane % 64 < 32, -1.0, 1.0)[None, :]
    return np.cos(angles).astype(np.float32), (np.sin(angles) * sign).astype(np.float32)


def body(
    inputs, cotangent, segments, routes, mixer_gain, query_weight, key_matrix, value_matrix, out_weight,
    expert_gain, router_weight, gate_weight, up_weight, down_weight,
):
    start = inputs.reshape(TOKENS, WIDTH)
    loss = cotangent.reshape(TOKENS, WIDTH)
    small_mine = jnp.concatenate(
        [mixer_gain, expert_gain, jnp.transpose(router_weight[0]), jnp.zeros((11, 512), BF16)], axis=0
    )
    mine = (
        query_weight[0], key_matrix[0], value_matrix[0], out_weight[0], gate_weight[0], up_weight[0],
        down_weight[0],
    )
    *others, small_other = exchange(*mine, small_mine)
    weights = (mine, tuple(others))
    small = (small_mine, small_other)
    seg = segments[:, 0]
    place = jnp.arange(128, dtype=jnp.int32)
    allowed = (seg[:, :, None] == seg[:, None, :]) & (place[None, None, :] <= place[None, :, None])
    bias = jnp.where(allowed, 0.0, -1e30).astype(F32)
    picks = routes.reshape(TOKENS, 2)
    columns = jnp.arange(16, dtype=jnp.int32)[None, :] - 2
    marks = ((picks[:, 0:1] == columns) | (picks[:, 1:2] == columns)).astype(F32)
    cos, sin = (jnp.asarray(table) for table in rotary_tables())

    (relay,) = forward(start, start, bias, marks, cos, sin, small, weights, False)
    received = lax.ppermute(relay, "section", [(0, 1)])
    relay, out, *kept = forward(start, received, bias, marks, cos, sin, small, weights, True)
    (relay,) = backward(loss, loss, cos, sin, small, kept, weights, False)
    returned = lax.ppermute(relay, "section", [(1, 0)])
    relay, grad, small_grad, up, bgu, bb, bqkv = backward(
        returned, loss, cos, sin, small, kept, weights, True
    )
    pieces = (kept[1], kept[6], kept[8], kept[12], up, bgu, bb, bqkv)
    owned = unpack(*reduce_gradients(pieces, small_grad))
    return (
        out.reshape(1, 2, 1, 128, WIDTH),
        grad.reshape(1, 2, 1, 128, WIDTH),
        owned[0],
    ) + tuple(item[None] for item in owned[1:5]) + (owned[5],) + tuple(item[None] for item in owned[6:])


def solution(mesh):
    return jax.shard_map(
        body,
        mesh=mesh,
        in_specs=(
            P(None, ("shard", "replica"), None, None),
            P(None, ("shard", "replica"), None, None),
            P(None, ("shard", "replica"), None),
            P("section", None, ("shard", "replica"), None, None),
            P("section", "shard"),
            P("section", "shard", None),
            P("section", "shard", None),
            P("section", "shard", None),
            P("section", "shard", None),
            P("section", "shard"),
            P("section", "shard", None),
            P("section", None, "shard", None),
            P("section", None, "shard", None),
            P("section", None, "shard", None),
        ),
        out_specs=(
            P("section", None, ("shard", "replica"), None, None),
            P("section", None, ("shard", "replica"), None, None),
            P("section", "shard"),
            P("section", "shard", None),
            P("section", "shard", None),
            P("section", "shard", None),
            P("section", "shard", None),
            P("section", "shard"),
            P("section", "shard", None),
            P("section", None, "shard", None),
            P("section", None, "shard", None),
            P("section", None, "shard", None),
        ),
        check_vma=False,
    )
```

```python
import functools

import numpy as np
import jax
import jax.numpy as jnp
from jax import lax
from jax.experimental import pallas as pl
from jax.experimental.pallas import tpu as pltpu
from jax.sharding import PartitionSpec as P

EPSILON = 1e-06
NT = (((1,), (1,)), ((), ()))
NN = (((1,), (0,)), ((), ()))
TN = (((0,), (0,)), ((), ()))
F32 = jnp.float32
BF16 = jnp.bfloat16
TOKENS = 256
WIDTH = 1024
VMEM_LIMIT = 62 * 1024 * 1024
MESH = pl.DeviceIdType.MESH
ROWS = 7680
COLS = 512
PARTS = 5
PART = ROWS // PARTS
DIMS = 5
KEY, VALUE, OUT, EXPERT, DOWN = 1024, 1536, 2048, 3072, 6144
PIECES = ((0, 1024), (1024, 1024), (2048, 1024), (3072, 1536), (4608, 1536), (6144, 1536))


def dot(a, b, dims):
    return lax.dot_general(a, b, dims, preferred_element_type=F32)


def scale_of(rows):
    return lax.rsqrt(jnp.mean(rows * rows, axis=-1, keepdims=True) + EPSILON)


def swap_halves(u):
    lanes = u.shape[1]
    lane = lax.broadcasted_iota(jnp.int32, u.shape, 1)
    return jnp.where(lane % 64 < 32, pltpu.roll(u, lanes - 32, 1), pltpu.roll(u, 32, 1))


def low_half(shape):
    return lax.broadcasted_iota(jnp.int32, shape, 1) < 64


def both_ways(block):
    wide = block.astype(F32)
    turned = pltpu.roll(wide, 64, 1)
    low = low_half(wide.shape)
    return jnp.where(low, wide, turned).astype(BF16), jnp.where(low, turned, wide).astype(BF16)


def stack_heads(block):
    wide = block.astype(F32)
    low = low_half(wide.shape)
    zero = jnp.zeros_like(wide)
    return jnp.concatenate([jnp.where(low, wide, zero), jnp.where(low, zero, wide)], axis=0).astype(BF16)


def join_heads(rows):
    return jnp.where(low_half((128, 128)), rows[:128], rows[128:])


def norm_back(rows, scale, gain, incoming):
    weighted = incoming * gain
    gain_part = jnp.sum(incoming * rows * scale, axis=0, keepdims=True)
    part = scale * weighted - rows * (scale * scale * scale) * jnp.mean(weighted * rows, axis=-1, keepdims=True)
    return part, gain_part


def cube_position():
    r = lax.axis_index("replica")
    x = r % 4
    z = (r // 4) % 4
    y = r // 16
    bits = (((x + 1) // 2) % 2, x // 2, ((z + 1) // 2) % 2, z // 2, y)
    partners = (
        r + 1 - 2 * (x % 2),
        r + 3 - 2 * x,
        r + 4 - 8 * (z % 2),
        r + 12 - 8 * z,
        (r + 16) % 32,
    )
    return bits, partners


def rows_at(at, count):
    if isinstance(at, int):
        return pl.ds(at, count)
    return pl.ds(pl.multiple_of(at, 16), count)


def add_rows(dst, dst_at, a, a_at, b, b_at, count):
    step = min(count, 192)

    def one(i, carry):
        at = i * step
        dst[rows_at(dst_at + at, step), :] = (
            a[rows_at(a_at + at, step), :] + b[rows_at(b_at + at, step), :]
        )
        return carry

    lax.fori_loop(0, count // step, one, 0)


def remote_copy(source, target, send_sem, recv_sem, device):
    return pltpu.make_async_remote_copy(
        src_ref=source, dst_ref=target, send_sem=send_sem, recv_sem=recv_sem,
        device_id=device, device_id_type=MESH,
    )


def layer_kernel(
    start_ref, loss_ref, segment_ref, route_ref, mixer_ref, expert_ref, router_ref, cos_ref, sin_ref,
    query_hbm, key_hbm, value_hbm, out_hbm, gate_hbm, up_hbm, down_hbm,
    output_hbm, gradient_hbm, total_hbm, small_out,
    pool, from_core, from_cube, whole, small_pair, small_mine, small_held, small_got,
    relayed, returned, relay, output, bias_ref,
    hidden_ref, normed_ref, q_ref, k_ref, v_ref, p_ref, att_ref, middle_ref, ne_ref, gl_ref, ul_ref, gi_ref,
    up_ref, bgu_ref, bb_ref, bqkv_ref, bne_ref, bm_ref, ba_ref, gradient,
    load_sem, weight_send, weight_recv, pair_send, pair_recv, relay_send, relay_recv,
    core_send, core_recv, cube_send, cube_recv, share_send, share_recv, small_send, small_recv, store_sem,
    output_sem,
):
    core = lax.axis_index("shard")
    section = lax.axis_index("section")
    bits, partners = cube_position()
    sibling = {"shard": 1 - core}
    other = {"section": 1 - section}

    barrier = pltpu.get_barrier_semaphore()
    pl.semaphore_signal(barrier, inc=1, device_id=sibling, device_id_type=MESH)
    pl.semaphore_signal(barrier, inc=1, device_id=other, device_id_type=MESH)
    for partner in partners:
        pl.semaphore_signal(barrier, inc=1, device_id={"replica": partner}, device_id_type=MESH)

    work = pool.at[core]
    loads = []

    def load(source, at, count):
        copy = pltpu.make_async_copy(source, work.at[pl.ds(at, count)], load_sem.at[len(loads)])
        copy.start()
        loads.append(copy)

    for i in range(2):
        load(query_hbm.at[:, pl.ds(i * 512, 512)], i * 512, 512)
    load(key_hbm, KEY, 512)
    load(value_hbm, VALUE, 512)
    for i in range(2):
        load(out_hbm.at[:, pl.ds(i * 512, 512)], OUT + i * 512, 512)
    for e in range(3):
        load(gate_hbm.at[e], EXPERT + e * 1024, 512)
        load(up_hbm.at[e], EXPERT + e * 1024 + 512, 512)
    for e in range(3):
        for i in range(2):
            load(down_hbm.at[e, :, pl.ds(i * 512, 512)], DOWN + e * 512 + i * 256, 256)
    needed = ((0, 1), (2, 3), (4, 5), (6, 7, 8), (9, 10, 11), (12, 13, 14, 15, 16, 17))

    pick = lax.broadcasted_iota(jnp.int32, (16, 3), 0) == lax.broadcasted_iota(jnp.int32, (16, 3), 1) + 2
    turned_router = dot(jnp.where(pick, 1.0, 0.0).astype(BF16), router_ref[...], NN)
    row = lax.broadcasted_iota(jnp.int32, (16, 512), 0)
    mixed = jnp.where(
        row == 0, mixer_ref[...].astype(F32), jnp.where(row == 1, expert_ref[...].astype(F32), turned_router)
    )
    small_pair[core] = mixed.astype(BF16)

    pl.semaphore_wait(barrier, 2 + DIMS)
    sends = []

    def remote(source, target, send_sem, recv_sem, device):
        copy = remote_copy(source, target, send_sem, recv_sem, device)
        copy.start()
        sends.append(copy)
        return copy

    pair = remote(small_pair.at[core], small_pair.at[core], pair_send, pair_recv, sibling)
    given = []

    def give():
        i = len(given)
        if i < len(PIECES):
            for index in needed[i]:
                loads[index].wait()
            rows = pl.ds(*PIECES[i])
            given.append(remote(work.at[rows], work.at[rows], weight_send.at[i], weight_recv.at[i], sibling))

    give()
    give()

    def arrive(i):
        given[i].wait_recv()
        give()

    position = lax.broadcasted_iota(jnp.int32, (128, 128), 0)
    earlier = lax.broadcasted_iota(jnp.int32, (128, 128), 1) <= position
    for pack in range(2):
        across = jnp.broadcast_to(segment_ref[pack:pack + 1, :].astype(F32), (128, 128))
        allowed = (across == jnp.transpose(across)) & earlier
        bias_ref[pack] = jnp.where(allowed, 0.0, -1e30)
    lane = lax.broadcasted_iota(jnp.int32, (TOKENS, 16), 1)
    expert_row = lax.broadcasted_iota(jnp.int32, (16, 128), 0)
    picked = []
    for pack in range(2):
        hit = (route_ref[pack, 0:1] + 2 == expert_row) | (route_ref[pack, 1:2] + 2 == expert_row)
        picked.append(jnp.transpose(jnp.where(hit, 1.0, 0.0)))
    marks = jnp.concatenate(picked, axis=0) > 0.0

    relays = [
        remote_copy(relay.at[i], relayed.at[i], relay_send.at[i], relay_recv.at[i], other) for i in range(2)
    ]
    returns = [
        remote_copy(relay.at[i], returned.at[i], relay_send.at[2 + i], relay_recv.at[2 + i], other)
        for i in range(2)
    ]

    @pl.when(section == 0)
    def _():
        hidden_ref[...] = start_ref[...]

    @pl.when(section == 1)
    def _():
        for i in range(2):
            relays[i].wait_recv()
            hidden_ref[:, i * 512:(i + 1) * 512] = relayed[i]

    pair.wait_recv()
    small = jnp.concatenate([small_pair[0], small_pair[1]], axis=1)
    x = hidden_ref[...].astype(F32)
    normed_ref[...] = (x * scale_of(x) * small[0:1].astype(F32)).astype(BF16)

    def through(a_ref, at, lanes):
        return dot(a_ref[:, 0:512], pool[0, at:at + 512, lanes], NN) + dot(
            a_ref[:, 512:1024], pool[1, at:at + 512, lanes], NN
        )

    quarters = (slice(0, 256), slice(256, 512))
    for j, (target, at, turned) in enumerate(
        ((q_ref, 0, True), (q_ref, 512, True), (k_ref, 0, True), (v_ref, 0, False))
    ):
        if j % 2 == 0:
            arrive(j // 2)
        for lanes in quarters:
            u = through(normed_ref, j * 512, lanes)
            if turned:
                u = u * cos_ref[...] + swap_halves(u) * sin_ref[...]
            target[:, at + lanes.start:at + lanes.stop] = u.astype(BF16)

    for pack in range(2):
        rows = slice(pack * 128, pack * 128 + 128)
        bias = jnp.concatenate([bias_ref[pack], bias_ref[pack]], axis=0)
        for pair_at in range(4):
            keys = both_ways(k_ref[rows, pair_at * 128:(pair_at + 1) * 128])
            values = both_ways(v_ref[rows, pair_at * 128:(pair_at + 1) * 128])
            for half in range(2):
                g = pair_at * 2 + half
                queries = stack_heads(q_ref[rows, g * 128:(g + 1) * 128])
                scores = dot(queries, keys[half], NT) * 0.125 + bias
                exponent = jnp.exp(scores - jnp.max(scores, axis=-1, keepdims=True))
                attention = (exponent / jnp.sum(exponent, axis=-1, keepdims=True)).astype(BF16)
                p_ref[pack, g] = attention
                att_ref[rows, g * 128:(g + 1) * 128] = join_heads(dot(attention, values[half], NN)).astype(BF16)

    arrive(2)
    for i in range(4):
        cols = slice(i * 256, (i + 1) * 256)
        middle_ref[:, cols] = hidden_ref[:, cols].astype(F32) + through(
            att_ref, OUT + (i // 2) * 512, quarters[i % 2]
        )
    middle = middle_ref[...]
    ne_ref[...] = (middle * scale_of(middle) * small[1:2].astype(F32)).astype(BF16)
    logits = dot(ne_ref[...], small, NT)
    peak = jnp.max(jnp.where(marks, logits, -1e30), axis=-1, keepdims=True)
    lifted = jnp.where(marks, jnp.exp(jnp.where(marks, logits - peak, 0.0)), 0.0)
    gates = lifted / jnp.sum(lifted, axis=-1, keepdims=True)

    for e in range(3):
        if e < 2:
            arrive(3 + e)
        for lanes in quarters:
            flat = slice(e * 512 + lanes.start, e * 512 + lanes.stop)
            gl = through(ne_ref, EXPERT + e * 1024, lanes)
            ul = through(ne_ref, EXPERT + e * 1024 + 512, lanes)
            gl_ref[:, flat] = gl.astype(BF16)
            ul_ref[:, flat] = ul.astype(BF16)
            inner = gl * jax.nn.sigmoid(gl) * ul
            gi_ref[:, flat] = (gates[:, 2 + e:3 + e] * inner).astype(BF16)

    arrive(5)
    for i in range(4):
        cols = slice(i * 256, (i + 1) * 256)
        total = middle_ref[:, cols]
        for e in range(3):
            at = DOWN + e * 512 + (i // 2) * 256
            for h in range(2):
                total = total + dot(
                    gi_ref[:, e * 512 + h * 256:e * 512 + (h + 1) * 256],
                    pool[h, at:at + 256, quarters[i % 2]], NN,
                )
        output[:, cols] = total
        relay[i // 2, :, quarters[i % 2]] = total.astype(BF16)
        if i % 2 == 1:
            @pl.when(section == 0)
            def _():
                relays[i // 2].start()

    output_copy = pltpu.make_async_copy(output, output_hbm, output_sem.at[0])
    output_copy.start()

    @pl.when(section == 0)
    def _():
        for i in range(2):
            relays[i].wait_send()
        for i in range(2):
            returns[i].wait_recv()
            up_ref[:, i * 512:(i + 1) * 512] = returned[i]

    @pl.when(section == 1)
    def _():
        up_ref[...] = loss_ref[...]

    pulls = jnp.zeros((TOKENS, 16), F32)
    for e in range(3):
        gate = gates[:, 2 + e:3 + e]
        for h in range(2):
            flat = slice(e * 512 + h * 256, e * 512 + (h + 1) * 256)
            at = DOWN + e * 512
            u = dot(up_ref[:, 0:512], pool[h, at:at + 256, :], NT) + dot(
                up_ref[:, 512:1024], pool[h, at + 256:at + 512, :], NT
            )
            gl = gl_ref[:, flat].astype(F32)
            ul = ul_ref[:, flat].astype(F32)
            sg = jax.nn.sigmoid(gl)
            silu = gl * sg
            pulls = pulls + jnp.where(lane == 2 + e, jnp.sum(u * silu * ul, axis=-1, keepdims=True), 0.0)
            inner = gate * u
            at = e * 1024 + h * 256
            bgu_ref[:, at:at + 256] = (inner * ul * sg * (1.0 + gl * (1.0 - sg))).astype(BF16)
            bgu_ref[:, at + 512:at + 768] = (inner * silu).astype(BF16)
    back_logits = (gates * (pulls - jnp.sum(gates * pulls, axis=-1, keepdims=True))).astype(BF16)

    for i in range(4):
        cols = slice(i * 256, (i + 1) * 256)
        h, inside = i // 2, (i % 2) * 256
        total = dot(back_logits, small[:, cols], NN)
        for j in range(6):
            at = EXPERT + j * 512 + inside
            total = total + dot(bgu_ref[:, j * 512:(j + 1) * 512], pool[h, at:at + 256, :], NT)
        bne_ref[:, cols] = total
    middle = middle_ref[...]
    part, expert_gain = norm_back(middle, scale_of(middle), small[1:2].astype(F32), bne_ref[...])
    bm_ref[...] = up_ref[...].astype(F32) + part
    bb_ref[...] = bm_ref[...].astype(BF16)

    for i in range(4):
        h, inside = i // 2, (i % 2) * 256
        total = dot(bb_ref[:, 0:512], pool[h, OUT + inside:OUT + inside + 256, :], NT)
        total = total + dot(bb_ref[:, 512:1024], pool[h, OUT + 512 + inside:OUT + inside + 768, :], NT)
        ba_ref[:, i * 256:(i + 1) * 256] = total.astype(BF16)

    cos, sin = cos_ref[0:128, 0:128], sin_ref[0:128, 0:128]

    def unturn(u):
        return (u * cos - swap_halves(u) * sin).astype(BF16)

    low = low_half((128, 128))
    for pack in range(2):
        rows = slice(pack * 128, pack * 128 + 128)
        for pair_at in range(4):
            keys = both_ways(k_ref[rows, pair_at * 128:(pair_at + 1) * 128])
            values = both_ways(v_ref[rows, pair_at * 128:(pair_at + 1) * 128])
            back_k, back_v = [], []
            for half in range(2):
                g = pair_at * 2 + half
                cols = slice(g * 128, (g + 1) * 128)
                queries = stack_heads(q_ref[rows, cols])
                back_out = stack_heads(ba_ref[rows, cols])
                attention = p_ref[pack, g]
                wide = attention.astype(F32)
                pull = dot(back_out, values[half], NT)
                bv = dot(attention, back_out, TN)
                back_v.append(bv + pltpu.roll(bv, 64, 1))
                spread = wide * pull
                back_scores = (
                    (spread - wide * jnp.sum(spread, axis=-1, keepdims=True)) * 0.125
                ).astype(BF16)
                bqkv_ref[rows, cols] = unturn(join_heads(dot(back_scores, keys[half], NN)))
                bk = dot(back_scores, queries, TN)
                back_k.append(bk + pltpu.roll(bk, 64, 1))
            at = 1024 + pair_at * 128
            bqkv_ref[rows, at:at + 128] = unturn(jnp.where(low, back_k[0], back_k[1]))
            bqkv_ref[rows, at + 512:at + 640] = jnp.where(low, back_v[0], back_v[1]).astype(BF16)

    for i in range(4):
        h, inside = i // 2, (i % 2) * 256
        total = jnp.zeros((TOKENS, 256), F32)
        for j in range(4):
            at = j * 512 + inside
            total = total + dot(bqkv_ref[:, j * 512:(j + 1) * 512], pool[h, at:at + 256, :], NT)
        bne_ref[:, i * 256:(i + 1) * 256] = total
    x = hidden_ref[...].astype(F32)
    part, mixer_gain = norm_back(x, scale_of(x), small[0:1].astype(F32), bne_ref[...])
    gradient[...] = bm_ref[...] + part
    for i in range(2):
        relay[i] = gradient[:, i * 512:(i + 1) * 512].astype(BF16)

    @pl.when(section == 1)
    def _():
        for i in range(2):
            returns[i].start()

    gradient_copy = pltpu.make_async_copy(gradient, gradient_hbm, output_sem.at[1])
    gradient_copy.start()
    router = dot(back_logits, ne_ref[...], TN)
    row = lax.broadcasted_iota(jnp.int32, router.shape, 0)
    mixed = jnp.where(row == 0, mixer_gain, jnp.where(row == 1, expert_gain, router))
    small_mine[0] = mixed[:, 0:512]
    small_mine[1] = mixed[:, 512:1024]

    def tiles(p, half):
        def tile(a, a_at, count, b, b_at, at):
            rows = a[:, pl.ds(pl.multiple_of(a_at, 256), count)]
            pool[half, at:at + count, :] = dot(rows, b[:, b_at:b_at + 512], TN).astype(BF16)

        left = half * 512
        if p == 0:
            for i in range(3):
                tile(normed_ref, left, 512, bqkv_ref, i * 512, i * 512)
        elif p == 1:
            tile(normed_ref, left, 512, bqkv_ref, 1536, VALUE)
            for i in range(2):
                tile(att_ref, left, 512, bb_ref, i * 512, OUT + i * 512)
        elif p < 4:
            for i in range(3 * p - 6, 3 * p - 3):
                tile(ne_ref, left, 512, bgu_ref, i * 512, EXPERT + i * 512)
        else:
            for e in range(3):
                for i in range(2):
                    tile(gi_ref, e * 512 + half * 256, 256, up_ref, i * 512, DOWN + e * 512 + i * 256)

    for copy in sends:
        copy.wait_send()
    sends.clear()
    lent = pool.at[1 - core]
    size = [PART >> s for s in range(DIMS + 1)]
    bit = [[bits[(p + s) % DIMS] for s in range(DIMS)] for p in range(PARTS)]
    device = [[{"replica": partners[(p + s) % DIMS]} for s in range(DIMS)] for p in range(PARTS)]
    held = [[p * PART] for p in range(PARTS)]
    for p in range(PARTS):
        for s in range(DIMS):
            held[p].append(held[p][s] + bit[p][s] * size[s + 1])

    def away(p, s):
        return held[p][s] + (1 - bit[p][s]) * size[s + 1]

    def core_piece(p, piece):
        at = away(p, 0) if piece == 0 else held[p][1]
        rows = rows_at(at, size[1])
        return remote(
            lent.at[rows], from_core.at[rows], core_send.at[2 * p + piece], core_recv.at[2 * p + piece], sibling
        )

    def slot(p, s, piece):
        return p * PART + PART - size[s] + piece * size[s + 2]

    def scatter(p, s):
        copies = []
        for piece in range(2 if s < DIMS - 1 else 1):
            index = (p * DIMS + s) * 2 + piece
            if s < DIMS - 1:
                b = bit[p][s + 1]
                at = away(p, s) + ((1 - b) if piece == 0 else b) * size[s + 2]
                count = size[s + 2]
                into = slot(p, s, piece)
            else:
                at, count, into = away(p, s), size[s + 1], p * PART + PART - size[s]
            copies.append(remote(
                work.at[rows_at(at, count)], from_cube.at[rows_at(into, count)],
                cube_send.at[index], cube_recv.at[index], device[p][s],
            ))
        return copies

    def share(p, s, at, piece):
        count = size[s + 2] if s < DIMS - 1 else size[DIMS]
        index = (p * DIMS + s) * 2 + piece
        rows = rows_at(at, count)
        return remote(whole.at[rows], whole.at[rows], share_send.at[index], share_recv.at[index], device[p][s])

    stores = []

    def store(at, count):
        rows = rows_at(at, count)
        copy = pltpu.make_async_copy(whole.at[rows], total_hbm.at[rows], store_sem.at[len(stores)])
        copy.start()
        stores.append(copy)

    small_copy = remote(small_mine.at[1 - core], small_got.at[0], small_send.at[0], small_recv.at[0], sibling)
    first = [None] * PARTS
    cube = [None] * PARTS

    def begin(p):
        first[p].wait_recv()
        at = away(p, 0)
        add_rows(work, at, work, at, from_core, at, size[1])
        cube[p] = scatter(p, 0)

    for p in range(PARTS):
        tiles(p, 1 - core)
        first[p] = core_piece(p, 0)
        tiles(p, core)
        if p > 0:
            begin(p - 1)
    second = [core_piece(p, 1) for p in range(PARTS)]
    begin(PARTS - 1)
    small_copy.wait_recv()
    small_held[0] = small_mine[core] + small_got[0]
    small_copy = remote(
        small_held.at[0], small_got.at[1], small_send.at[1], small_recv.at[1], {"replica": partners[0]}
    )
    for p in range(PARTS):
        second[p].wait_recv()
        at = held[p][1]
        add_rows(work, at, work, at, from_core, at, size[1])

    shared = [None] * PARTS
    for s in range(DIMS):
        later = [None] * PARTS
        for p in range(PARTS):
            copies = cube[p]
            copies[0].wait_recv()
            if s < DIMS - 1:
                at = away(p, s + 1)
                add_rows(work, at, work, at, from_cube, slot(p, s, 0), size[s + 2])
                later[p] = copies[1]
                cube[p] = scatter(p, s + 1)
            else:
                at = held[p][DIMS]
                add_rows(whole, at, work, at, from_cube, p * PART + PART - size[s], size[DIMS])
                shared[p] = {(s, 0): share(p, s, at, 0), (s - 1, 0): share(p, s - 1, at, 0)}
                store(at, size[DIMS])
        if s < DIMS - 1:
            for p in range(PARTS):
                later[p].wait_recv()
                at = held[p][s + 2]
                add_rows(work, at, work, at, from_cube, slot(p, s, 1), size[s + 2])
        small_copy.wait_recv()
        if s < DIMS - 1:
            small_held[s + 1] = small_held[s] + small_got[s + 1]
            small_copy = remote(
                small_held.at[s + 1], small_got.at[s + 2], small_send.at[s + 2], small_recv.at[s + 2],
                {"replica": partners[s + 1]},
            )
        else:
            small_out[...] = small_held[s] + small_got[s + 1]

    for s in reversed(range(DIMS)):
        for p in range(PARTS):
            shared[p][(s, 0)].wait_recv()
            if s < DIMS - 1:
                shared[p][(s, 1)].wait_recv()
            got = away(p, s)
            if s > 0:
                shared[p][(s - 1, 1)] = share(p, s - 1, got, 1)
            if s > 1:
                shared[p][(s - 2, 0)] = share(p, s - 2, held[p][s], 0)
            store(got, size[s + 1])

    @pl.when(section == 1)
    def _():
        for i in range(2):
            returns[i].wait_send()

    for copy in sends:
        copy.wait_send()
    for copy in stores:
        copy.wait()
    output_copy.wait()
    gradient_copy.wait()


def specs(places):
    return [pl.BlockSpec(memory_space=place) for place in places]


def both_layers(operands, weights):
    dma = pltpu.SemaphoreType.DMA
    wide, narrow = pltpu.VMEM((TOKENS, WIDTH), F32), pltpu.VMEM((TOKENS, WIDTH), BF16)
    halves = pltpu.VMEM((2, TOKENS, 512), BF16)
    buffer = pltpu.VMEM((ROWS, COLS), BF16)
    inner = pltpu.VMEM((TOKENS, 1536), BF16)
    return pl.pallas_call(
        layer_kernel,
        out_shape=(
            jax.ShapeDtypeStruct((TOKENS, WIDTH), F32),
            jax.ShapeDtypeStruct((TOKENS, WIDTH), F32),
            jax.ShapeDtypeStruct((ROWS, COLS), BF16),
            jax.ShapeDtypeStruct((16, COLS), F32),
        ),
        in_specs=specs([pltpu.VMEM] * len(operands) + [pl.ANY] * len(weights)),
        out_specs=tuple(specs([pl.ANY, pl.ANY, pl.ANY, pltpu.VMEM])),
        scratch_shapes=[
            pltpu.VMEM((2, ROWS, COLS), BF16), buffer, buffer, buffer,
            pltpu.VMEM((2, 16, COLS), BF16), pltpu.VMEM((2, 16, COLS), F32),
            pltpu.VMEM((DIMS, 16, COLS), F32), pltpu.VMEM((DIMS + 1, 16, COLS), F32),
            halves, halves, halves, wide, pltpu.VMEM((2, 128, 128), F32),
            narrow, narrow, narrow, pltpu.VMEM((TOKENS, 512), BF16), pltpu.VMEM((TOKENS, 512), BF16),
            pltpu.VMEM((2, 8, 256, 128), BF16), narrow, wide, narrow, inner, inner, inner,
            narrow, pltpu.VMEM((TOKENS, 3072), BF16), narrow, pltpu.VMEM((TOKENS, 2048), BF16),
            wide, wide, narrow, wide,
            dma((18,)), dma((6,)), dma((6,)), dma, dma, dma((4,)), dma((4,)),
            dma((2 * PARTS,)), dma((2 * PARTS,)),
            dma((2 * PARTS * DIMS,)), dma((2 * PARTS * DIMS,)),
            dma((2 * PARTS * DIMS,)), dma((2 * PARTS * DIMS,)),
            dma((DIMS + 1,)), dma((DIMS + 1,)),
            dma((PARTS + PARTS * DIMS,)), dma((2,)),
        ],
        compiler_params=pltpu.CompilerParams(
            collective_id=1, has_side_effects=True, vmem_limit_bytes=VMEM_LIMIT
        ),
    )(*operands, *weights)


def unpack_kernel(
    total_ref, small_ref, output_ref, gradient_ref, mixer_ref, query_ref, key_ref, value_ref, out_ref,
    expert_ref, router_ref, gate_ref, up_ref, down_ref, output_out, gradient_out,
    got, wide, passed, load_sem, store_sem,
):
    loads = []
    for i in range(15):
        rows = pl.ds(i * 512, 512)
        copy = pltpu.make_async_copy(total_ref.at[rows], got.at[rows], load_sem.at[i])
        copy.start()
        loads.append(copy)
    passes = [
        pltpu.make_async_copy(source, passed.at[i], load_sem.at[15 + i])
        for i, source in enumerate((output_ref, gradient_ref))
    ]
    for copy in passes:
        copy.start()
    stores = []

    def send(source, target):
        copy = pltpu.make_async_copy(source, target, store_sem.at[len(stores)])
        copy.start()
        stores.append(copy)

    small = small_ref[...]
    mixer_ref[...] = small[0:1]
    expert_ref[...] = small[1:2]
    for i in range(3):
        router_ref[i] = small[2 + i:3 + i]

    def put(at, count, target):
        wide[at:at + count, :] = got[at:at + count, :].astype(F32)
        send(wide.at[pl.ds(at, count)], target)

    for i in range(15):
        loads[i].wait()
        at = i * 512
        cols = pl.ds((i % 2) * 512, 512)
        if i < 2:
            put(at, 512, query_ref.at[:, cols])
        elif i == 2:
            put(at, 512, key_ref)
        elif i == 3:
            put(at, 512, value_ref)
        elif i < 6:
            put(at, 512, out_ref.at[:, cols])
        elif i < 12:
            e, which = (i - 6) // 2, (i - 6) % 2
            put(at, 512, (up_ref if which else gate_ref).at[e])
        else:
            for j in range(2):
                put(at + j * 256, 256, down_ref.at[i - 12, :, pl.ds(j * 512, 512)])
    for i, target in enumerate((output_out, gradient_out)):
        passes[i].wait()
        send(passed.at[i], target)
    for copy in stores:
        copy.wait()


def unpack(total, small, output, gradient):
    shapes = (
        (1, 512), (512, 1024), (512, 512), (512, 512), (512, 1024), (1, 512), (3, 1, 512),
        (3, 512, 512), (3, 512, 512), (3, 256, 1024), (TOKENS, WIDTH), (TOKENS, WIDTH),
    )
    places = [pl.ANY if i not in (0, 5, 6) else pltpu.VMEM for i in range(12)]
    return pl.pallas_call(
        unpack_kernel,
        out_shape=tuple(jax.ShapeDtypeStruct(shape, F32) for shape in shapes),
        in_specs=specs([pl.ANY, pltpu.VMEM, pl.ANY, pl.ANY]),
        out_specs=tuple(specs(places)),
        scratch_shapes=[
            pltpu.VMEM((ROWS, COLS), BF16), pltpu.VMEM((ROWS, COLS), F32), pltpu.VMEM((2, TOKENS, WIDTH), F32),
            pltpu.SemaphoreType.DMA((17,)), pltpu.SemaphoreType.DMA((20,)),
        ],
        compiler_params=pltpu.CompilerParams(vmem_limit_bytes=VMEM_LIMIT),
    )(total, small, output, gradient)


def rotary_tables():
    lane = np.arange(256)
    frequency = np.power(10000.0, -2.0 * (lane % 32) / 64.0)
    angles = (np.arange(TOKENS) % 128)[:, None] * frequency[None, :]
    sign = np.where(lane % 64 < 32, -1.0, 1.0)[None, :]
    return np.cos(angles).astype(np.float32), (np.sin(angles) * sign).astype(np.float32)


def body(
    inputs, cotangent, segments, routes, mixer_gain, query_weight, key_matrix, value_matrix, out_weight,
    expert_gain, router_weight, gate_weight, up_weight, down_weight,
):
    cos, sin = (jnp.asarray(table) for table in rotary_tables())
    operands = (
        inputs.reshape(TOKENS, WIDTH), cotangent.reshape(TOKENS, WIDTH), segments.reshape(2, 128),
        jnp.swapaxes(routes[0, :, 0], 1, 2), mixer_gain, expert_gain, jnp.transpose(router_weight[0]), cos, sin,
    )
    weights = (
        query_weight[0], key_matrix[0], value_matrix[0], out_weight[0], gate_weight[0], up_weight[0],
        down_weight[0],
    )
    output, gradient, total, small = both_layers(operands, weights)
    *owned, output, gradient = unpack(total, small, output, gradient)
    return (
        output.reshape(1, 2, 1, 128, WIDTH),
        gradient.reshape(1, 2, 1, 128, WIDTH),
        owned[0],
    ) + tuple(item[None] for item in owned[1:5]) + (owned[5],) + (
        jnp.transpose(owned[6][:, 0])[None],
    ) + tuple(item[None] for item in owned[7:])


def solution(mesh):
    return jax.shard_map(
        body,
        mesh=mesh,
        in_specs=(
            P(None, ("shard", "replica"), None, None),
            P(None, ("shard", "replica"), None, None),
            P(None, ("shard", "replica"), None),
            P("section", None, ("shard", "replica"), None, None),
            P("section", "shard"),
            P("section", "shard", None),
            P("section", "shard", None),
            P("section", "shard", None),
            P("section", "shard", None),
            P("section", "shard"),
            P("section", "shard", None),
            P("section", None, "shard", None),
            P("section", None, "shard", None),
            P("section", None, "shard", None),
        ),
        out_specs=(
            P("section", None, ("shard", "replica"), None, None),
            P("section", None, ("shard", "replica"), None, None),
            P("section", "shard"),
            P("section", "shard", None),
            P("section", "shard", None),
            P("section", "shard", None),
            P("section", "shard", None),
            P("section", "shard"),
            P("section", "shard", None),
            P("section", None, "shard", None),
            P("section", None, "shard", None),
            P("section", None, "shard", None),
        ),
        check_vma=False,
    )
```

```python
import functools

import numpy as np
import jax
import jax.numpy as jnp
from jax import lax
from jax.experimental import pallas as pl
from jax.experimental.pallas import tpu as pltpu
from jax.sharding import PartitionSpec as P

EPSILON = 1e-06
NT = (((1,), (1,)), ((), ()))
NN = (((1,), (0,)), ((), ()))
TN = (((0,), (0,)), ((), ()))
F32 = jnp.float32
BF16 = jnp.bfloat16
TOKENS = 256
WIDTH = 1024
VMEM_LIMIT = 62 * 1024 * 1024
MESH = pl.DeviceIdType.MESH
ROWS = 7680
COLS = 512
PARTS = 5
PART = ROWS // PARTS
DIMS = 5
KEY, VALUE, OUT, EXPERT, DOWN = 1024, 1536, 2048, 3072, 6144
PIECES = ((0, 1024), (1024, 1024), (2048, 1024), (3072, 1536), (4608, 1536), (6144, 1536))


def dot(a, b, dims):
    return lax.dot_general(a, b, dims, preferred_element_type=F32)


def scale_of(rows):
    return lax.rsqrt(jnp.mean(rows * rows, axis=-1, keepdims=True) + EPSILON)


def swap_halves(u):
    lanes = u.shape[1]
    lane = lax.broadcasted_iota(jnp.int32, u.shape, 1)
    return jnp.where(lane % 64 < 32, pltpu.roll(u, lanes - 32, 1), pltpu.roll(u, 32, 1))


def low_half(shape):
    return lax.broadcasted_iota(jnp.int32, shape, 1) < 64


def both_ways(block):
    wide = block.astype(F32)
    turned = pltpu.roll(wide, 64, 1)
    low = low_half(wide.shape)
    return jnp.where(low, wide, turned).astype(BF16), jnp.where(low, turned, wide).astype(BF16)


def stack_heads(block):
    wide = block.astype(F32)
    low = low_half(wide.shape)
    zero = jnp.zeros_like(wide)
    return jnp.concatenate([jnp.where(low, wide, zero), jnp.where(low, zero, wide)], axis=0).astype(BF16)


def join_heads(rows):
    return jnp.where(low_half((128, 128)), rows[:128], rows[128:])


def norm_back(rows, scale, gain, incoming):
    weighted = incoming * gain
    gain_part = jnp.sum(incoming * rows * scale, axis=0, keepdims=True)
    part = scale * weighted - rows * (scale * scale * scale) * jnp.mean(weighted * rows, axis=-1, keepdims=True)
    return part, gain_part


def cube_position():
    r = lax.axis_index("replica")
    x = r % 4
    z = (r // 4) % 4
    y = r // 16
    bits = (((x + 1) // 2) % 2, x // 2, ((z + 1) // 2) % 2, z // 2, y)
    partners = (
        r + 1 - 2 * (x % 2),
        r + 3 - 2 * x,
        r + 4 - 8 * (z % 2),
        r + 12 - 8 * z,
        (r + 16) % 32,
    )
    return bits, partners


def rows_at(at, count):
    if isinstance(at, int):
        return pl.ds(at, count)
    return pl.ds(pl.multiple_of(at, 16), count)


def add_rows(dst, dst_at, a, a_at, b, b_at, count):
    step = min(count, 192)

    def one(i, carry):
        at = i * step
        dst[rows_at(dst_at + at, step), :] = (
            a[rows_at(a_at + at, step), :] + b[rows_at(b_at + at, step), :]
        )
        return carry

    lax.fori_loop(0, count // step, one, 0)


def remote_copy(source, target, send_sem, recv_sem, device):
    return pltpu.make_async_remote_copy(
        src_ref=source, dst_ref=target, send_sem=send_sem, recv_sem=recv_sem,
        device_id=device, device_id_type=MESH,
    )


def layer_kernel(
    start_ref, loss_ref, segment_ref, route_ref, mixer_ref, expert_ref, router_ref, cos_ref, sin_ref,
    query_hbm, key_hbm, value_hbm, out_hbm, gate_hbm, up_hbm, down_hbm,
    output_hbm, gradient_hbm, total_hbm, small_out,
    pool, from_core, from_cube, whole, small_pair, small_mine, small_held, small_got,
    relayed, returned, relay, output, bias_ref, mark_ref, gate_ref,
    hidden_ref, normed_ref, q_ref, k_ref, v_ref, p_ref, att_ref, middle_ref, ne_ref, gl_ref, ul_ref, gi_ref,
    up_ref, bgu_ref, bb_ref, bqkv_ref, bne_ref, bm_ref, ba_ref, gradient,
    load_sem, weight_send, weight_recv, pair_send, pair_recv, relay_send, relay_recv,
    core_send, core_recv, cube_send, cube_recv, share_send, share_recv, small_send, small_recv, store_sem,
    output_sem,
):
    core = lax.axis_index("shard")
    section = lax.axis_index("section")
    bits, partners = cube_position()
    sibling = {"shard": 1 - core}
    other = {"section": 1 - section}

    barrier = pltpu.get_barrier_semaphore()
    pl.semaphore_signal(barrier, inc=1, device_id=sibling, device_id_type=MESH)
    pl.semaphore_signal(barrier, inc=1, device_id=other, device_id_type=MESH)
    for partner in partners:
        pl.semaphore_signal(barrier, inc=1, device_id={"replica": partner}, device_id_type=MESH)

    work = pool.at[core]
    loads = []

    def load(source, at, count):
        copy = pltpu.make_async_copy(source, work.at[pl.ds(at, count)], load_sem.at[len(loads)])
        copy.start()
        loads.append(copy)

    for i in range(2):
        load(query_hbm.at[:, pl.ds(i * 512, 512)], i * 512, 512)
    load(key_hbm, KEY, 512)
    load(value_hbm, VALUE, 512)
    for i in range(2):
        load(out_hbm.at[:, pl.ds(i * 512, 512)], OUT + i * 512, 512)
    for e in range(3):
        load(gate_hbm.at[e], EXPERT + e * 1024, 512)
        load(up_hbm.at[e], EXPERT + e * 1024 + 512, 512)
    for e in range(3):
        for i in range(2):
            load(down_hbm.at[e, :, pl.ds(i * 512, 512)], DOWN + e * 512 + i * 256, 256)
    needed = ((0, 1), (2, 3), (4, 5), (6, 7, 8), (9, 10, 11), (12, 13, 14, 15, 16, 17))

    pick = lax.broadcasted_iota(jnp.int32, (16, 3), 0) == lax.broadcasted_iota(jnp.int32, (16, 3), 1) + 2
    turned_router = dot(jnp.where(pick, 1.0, 0.0).astype(BF16), router_ref[...], NN)
    row = lax.broadcasted_iota(jnp.int32, (16, 512), 0)
    mixed = jnp.where(
        row == 0, mixer_ref[...].astype(F32), jnp.where(row == 1, expert_ref[...].astype(F32), turned_router)
    )
    small_pair[core] = mixed.astype(BF16)

    pl.semaphore_wait(barrier, 2 + DIMS)
    sends = []

    def remote(source, target, send_sem, recv_sem, device):
        copy = remote_copy(source, target, send_sem, recv_sem, device)
        copy.start()
        sends.append(copy)
        return copy

    pair = remote(small_pair.at[core], small_pair.at[core], pair_send, pair_recv, sibling)
    given = []
    for i, (at, count) in enumerate(PIECES):
        rows = pl.ds(at, count)
        given.append(
            remote_copy(work.at[rows], work.at[rows], weight_send.at[i], weight_recv.at[i], sibling)
        )

    def give(i):
        if i < len(PIECES):
            for index in needed[i]:
                loads[index].wait()
            given[i].start()

    def arrive(i):
        given[i].wait_recv()
        give(i + 2)

    give(0)
    give(1)

    position = lax.broadcasted_iota(jnp.int32, (128, 128), 0)
    earlier = lax.broadcasted_iota(jnp.int32, (128, 128), 1) <= position
    for pack in range(2):
        across = jnp.broadcast_to(segment_ref[pack:pack + 1, :].astype(F32), (128, 128))
        allowed = (across == jnp.transpose(across)) & earlier
        bias_ref[pack] = jnp.where(allowed, 0.0, -1e30)
    lane = lax.broadcasted_iota(jnp.int32, (TOKENS, 16), 1)
    expert_row = lax.broadcasted_iota(jnp.int32, (16, 128), 0)
    picked = []
    for pack in range(2):
        hit = (route_ref[pack, 0:1] + 2 == expert_row) | (route_ref[pack, 1:2] + 2 == expert_row)
        picked.append(jnp.transpose(jnp.where(hit, 1.0, 0.0)))
    marks = jnp.concatenate(picked, axis=0) > 0.0

    relays = [
        remote_copy(relay.at[i], relayed.at[i], relay_send.at[i], relay_recv.at[i], other) for i in range(2)
    ]
    returns = [
        remote_copy(relay.at[i], returned.at[i], relay_send.at[2 + i], relay_recv.at[2 + i], other)
        for i in range(2)
    ]

    pair.wait_recv()
    small = jnp.concatenate([small_pair[0], small_pair[1]], axis=1)
    mark_ref[...] = jnp.where(marks, 1.0, 0.0)

    def through(a_ref, part, at, lanes):
        return dot(a_ref[part, 0:512], pool[0, at:at + 512, lanes], NN) + dot(
            a_ref[part, 512:1024], pool[1, at:at + 512, lanes], NN
        )

    quarters = (slice(0, 256), slice(256, 512))

    def forward(part, ready):
        x = hidden_ref[part, :].astype(F32)
        normed_ref[part, :] = (x * scale_of(x) * small[0:1].astype(F32)).astype(BF16)

        for j, (target, at, turned) in enumerate(
            ((q_ref, 0, True), (q_ref, 512, True), (k_ref, 0, True), (v_ref, 0, False))
        ):
            if j % 2 == 0:
                ready(j // 2)
            for lanes in quarters:
                u = through(normed_ref, part, j * 512, lanes)
                if turned:
                    u = u * cos_ref[part, :] + swap_halves(u) * sin_ref[part, :]
                target[part, at + lanes.start:at + lanes.stop] = u.astype(BF16)

        for pack in range(part.start // 128, part.stop // 128):
            rows = slice(pack * 128, pack * 128 + 128)
            bias = jnp.concatenate([bias_ref[pack], bias_ref[pack]], axis=0)
            for pair_at in range(4):
                keys = both_ways(k_ref[rows, pair_at * 128:(pair_at + 1) * 128])
                values = both_ways(v_ref[rows, pair_at * 128:(pair_at + 1) * 128])
                for half in range(2):
                    g = pair_at * 2 + half
                    queries = stack_heads(q_ref[rows, g * 128:(g + 1) * 128])
                    scores = dot(queries, keys[half], NT) * 0.125 + bias
                    exponent = jnp.exp(scores - jnp.max(scores, axis=-1, keepdims=True))
                    attention = (exponent / jnp.sum(exponent, axis=-1, keepdims=True)).astype(BF16)
                    p_ref[pack, g] = attention
                    att_ref[rows, g * 128:(g + 1) * 128] = join_heads(dot(attention, values[half], NN)).astype(BF16)

        ready(2)
        for i in range(4):
            cols = slice(i * 256, (i + 1) * 256)
            middle_ref[part, cols] = hidden_ref[part, cols].astype(F32) + through(
                att_ref, part, OUT + (i // 2) * 512, quarters[i % 2]
            )
        middle = middle_ref[part, :]
        ne_ref[part, :] = (middle * scale_of(middle) * small[1:2].astype(F32)).astype(BF16)
        logits = dot(ne_ref[part, :], small, NT)
        marks = mark_ref[part, :] > 0.0
        peak = jnp.max(jnp.where(marks, logits, -1e30), axis=-1, keepdims=True)
        lifted = jnp.where(marks, jnp.exp(jnp.where(marks, logits - peak, 0.0)), 0.0)
        gates = lifted / jnp.sum(lifted, axis=-1, keepdims=True)
        gate_ref[part, :] = gates

        for e in range(3):
            if e < 2:
                ready(3 + e)
            for lanes in quarters:
                flat = slice(e * 512 + lanes.start, e * 512 + lanes.stop)
                gl = through(ne_ref, part, EXPERT + e * 1024, lanes)
                ul = through(ne_ref, part, EXPERT + e * 1024 + 512, lanes)
                gl_ref[part, flat] = gl.astype(BF16)
                ul_ref[part, flat] = ul.astype(BF16)
                inner = gl * jax.nn.sigmoid(gl) * ul
                gi_ref[part, flat] = (gates[:, 2 + e:3 + e] * inner).astype(BF16)

        ready(5)
        for i in range(4):
            cols = slice(i * 256, (i + 1) * 256)
            total = middle_ref[part, cols]
            for e in range(3):
                at = DOWN + e * 512 + (i // 2) * 256
                for h in range(2):
                    total = total + dot(
                        gi_ref[part, e * 512 + h * 256:e * 512 + (h + 1) * 256],
                        pool[h, at:at + 256, quarters[i % 2]], NN,
                    )
            output[part, cols] = total
            for pack in range(part.start // 128, part.stop // 128):
                at = pack * 128 - part.start
                relay[pack, :, cols] = total[at:at + 128].astype(BF16)

    @pl.when(section == 0)
    def _():
        hidden_ref[...] = start_ref[...]
        forward(slice(0, TOKENS), arrive)
        for pack in range(2):
            relays[pack].start()
            relays[pack].wait_send()

    @pl.when(section == 1)
    def _():
        for i in range(len(PIECES)):
            arrive(i)
        for pack in range(2):
            part = slice(pack * 128, pack * 128 + 128)
            relays[pack].wait_recv()
            hidden_ref[part, :] = relayed[pack]
            forward(part, lambda i: None)

    output_copy = pltpu.make_async_copy(output, output_hbm, output_sem.at[0])
    output_copy.start()

    cos, sin = cos_ref[0:128, 0:128], sin_ref[0:128, 0:128]

    def unturn(u):
        return (u * cos - swap_halves(u) * sin).astype(BF16)

    low = low_half((128, 128))
    def backward(part):
        gates = gate_ref[part, :]
        lane = lax.broadcasted_iota(jnp.int32, (128, 16), 1)
        pulls = jnp.zeros((128, 16), F32)
        for e in range(3):
            gate = gates[:, 2 + e:3 + e]
            for h in range(2):
                flat = slice(e * 512 + h * 256, e * 512 + (h + 1) * 256)
                at = DOWN + e * 512
                u = dot(up_ref[part, 0:512], pool[h, at:at + 256, :], NT) + dot(
                    up_ref[part, 512:1024], pool[h, at + 256:at + 512, :], NT
                )
                gl = gl_ref[part, flat].astype(F32)
                ul = ul_ref[part, flat].astype(F32)
                sg = jax.nn.sigmoid(gl)
                silu = gl * sg
                pulls = pulls + jnp.where(lane == 2 + e, jnp.sum(u * silu * ul, axis=-1, keepdims=True), 0.0)
                inner = gate * u
                at = e * 1024 + h * 256
                bgu_ref[part, at:at + 256] = (inner * ul * sg * (1.0 + gl * (1.0 - sg))).astype(BF16)
                bgu_ref[part, at + 512:at + 768] = (inner * silu).astype(BF16)
        back_logits = (gates * (pulls - jnp.sum(gates * pulls, axis=-1, keepdims=True))).astype(BF16)

        for i in range(4):
            cols = slice(i * 256, (i + 1) * 256)
            h, inside = i // 2, (i % 2) * 256
            total = dot(back_logits, small[:, cols], NN)
            for j in range(6):
                at = EXPERT + j * 512 + inside
                total = total + dot(bgu_ref[part, j * 512:(j + 1) * 512], pool[h, at:at + 256, :], NT)
            bne_ref[part, cols] = total
        middle = middle_ref[part, :]
        change, expert_gain = norm_back(middle, scale_of(middle), small[1:2].astype(F32), bne_ref[part, :])
        bm_ref[part, :] = up_ref[part, :].astype(F32) + change
        bb_ref[part, :] = bm_ref[part, :].astype(BF16)

        for i in range(4):
            h, inside = i // 2, (i % 2) * 256
            total = dot(bb_ref[part, 0:512], pool[h, OUT + inside:OUT + inside + 256, :], NT)
            total = total + dot(bb_ref[part, 512:1024], pool[h, OUT + 512 + inside:OUT + inside + 768, :], NT)
            ba_ref[part, i * 256:(i + 1) * 256] = total.astype(BF16)

        for pack in (part.start // 128,):
            rows = slice(pack * 128, pack * 128 + 128)
            for pair_at in range(4):
                keys = both_ways(k_ref[rows, pair_at * 128:(pair_at + 1) * 128])
                values = both_ways(v_ref[rows, pair_at * 128:(pair_at + 1) * 128])
                back_k, back_v = [], []
                for half in range(2):
                    g = pair_at * 2 + half
                    cols = slice(g * 128, (g + 1) * 128)
                    queries = stack_heads(q_ref[rows, cols])
                    back_out = stack_heads(ba_ref[rows, cols])
                    attention = p_ref[pack, g]
                    wide = attention.astype(F32)
                    pull = dot(back_out, values[half], NT)
                    bv = dot(attention, back_out, TN)
                    back_v.append(bv + pltpu.roll(bv, 64, 1))
                    spread = wide * pull
                    back_scores = (
                        (spread - wide * jnp.sum(spread, axis=-1, keepdims=True)) * 0.125
                    ).astype(BF16)
                    bqkv_ref[rows, cols] = unturn(join_heads(dot(back_scores, keys[half], NN)))
                    bk = dot(back_scores, queries, TN)
                    back_k.append(bk + pltpu.roll(bk, 64, 1))
                at = 1024 + pair_at * 128
                bqkv_ref[rows, at:at + 128] = unturn(jnp.where(low, back_k[0], back_k[1]))
                bqkv_ref[rows, at + 512:at + 640] = jnp.where(low, back_v[0], back_v[1]).astype(BF16)

        for i in range(4):
            h, inside = i // 2, (i % 2) * 256
            total = jnp.zeros((128, 256), F32)
            for j in range(4):
                at = j * 512 + inside
                total = total + dot(bqkv_ref[part, j * 512:(j + 1) * 512], pool[h, at:at + 256, :], NT)
            bne_ref[part, i * 256:(i + 1) * 256] = total
        x = hidden_ref[part, :].astype(F32)
        change, mixer_gain = norm_back(x, scale_of(x), small[0:1].astype(F32), bne_ref[part, :])
        gradient[part, :] = bm_ref[part, :] + change
        relay[part.start // 128] = gradient[part, :].astype(BF16)
        router = dot(back_logits, ne_ref[part, :], TN)
        row = lax.broadcasted_iota(jnp.int32, router.shape, 0)
        return jnp.where(row == 0, mixer_gain, jnp.where(row == 1, expert_gain, router))

    mixed = jnp.zeros((16, WIDTH), F32)
    for pack in range(2):
        part = slice(pack * 128, pack * 128 + 128)

        @pl.when(section == 0)
        def _():
            returns[pack].wait_recv()
            up_ref[part, :] = returned[pack]

        @pl.when(section == 1)
        def _():
            up_ref[part, :] = loss_ref[part, :]

        mixed = mixed + backward(part)

        @pl.when(section == 1)
        def _():
            returns[pack].start()

    gradient_copy = pltpu.make_async_copy(gradient, gradient_hbm, output_sem.at[1])
    gradient_copy.start()
    small_mine[0] = mixed[:, 0:512]
    small_mine[1] = mixed[:, 512:1024]

    def tiles(p, half):
        def tile(a, a_at, count, b, b_at, at):
            rows = a[:, pl.ds(pl.multiple_of(a_at, 256), count)]
            pool[half, at:at + count, :] = dot(rows, b[:, b_at:b_at + 512], TN).astype(BF16)

        left = half * 512
        if p == 0:
            for i in range(3):
                tile(normed_ref, left, 512, bqkv_ref, i * 512, i * 512)
        elif p == 1:
            tile(normed_ref, left, 512, bqkv_ref, 1536, VALUE)
            for i in range(2):
                tile(att_ref, left, 512, bb_ref, i * 512, OUT + i * 512)
        elif p < 4:
            for i in range(3 * p - 6, 3 * p - 3):
                tile(ne_ref, left, 512, bgu_ref, i * 512, EXPERT + i * 512)
        else:
            for e in range(3):
                for i in range(2):
                    tile(gi_ref, e * 512 + half * 256, 256, up_ref, i * 512, DOWN + e * 512 + i * 256)

    for copy in given + [pair]:
        copy.wait_send()
    sends.clear()

    @pl.when(section == 1)
    def _():
        for i in range(2):
            returns[i].wait_send()

    lent = pool.at[1 - core]
    size = [PART >> s for s in range(DIMS + 1)]
    bit = [[bits[(p + s) % DIMS] for s in range(DIMS)] for p in range(PARTS)]
    device = [[{"replica": partners[(p + s) % DIMS]} for s in range(DIMS)] for p in range(PARTS)]
    held = [[p * PART] for p in range(PARTS)]
    for p in range(PARTS):
        for s in range(DIMS):
            held[p].append(held[p][s] + bit[p][s] * size[s + 1])

    def away(p, s):
        return held[p][s] + (1 - bit[p][s]) * size[s + 1]

    def core_piece(p, piece):
        at = away(p, 0) if piece == 0 else held[p][1]
        rows = rows_at(at, size[1])
        return remote(
            lent.at[rows], from_core.at[rows], core_send.at[2 * p + piece], core_recv.at[2 * p + piece], sibling
        )

    def slot(p, s, piece):
        return p * PART + PART - size[s] + piece * size[s + 2]

    def scatter(p, s):
        copies = []
        for piece in range(2 if s < DIMS - 1 else 1):
            index = (p * DIMS + s) * 2 + piece
            if s < DIMS - 1:
                b = bit[p][s + 1]
                at = away(p, s) + ((1 - b) if piece == 0 else b) * size[s + 2]
                count = size[s + 2]
                into = slot(p, s, piece)
            else:
                at, count, into = away(p, s), size[s + 1], p * PART + PART - size[s]
            copies.append(remote(
                work.at[rows_at(at, count)], from_cube.at[rows_at(into, count)],
                cube_send.at[index], cube_recv.at[index], device[p][s],
            ))
        return copies

    def share(p, s, at, piece):
        count = size[s + 2] if s < DIMS - 1 else size[DIMS]
        index = (p * DIMS + s) * 2 + piece
        rows = rows_at(at, count)
        return remote(whole.at[rows], whole.at[rows], share_send.at[index], share_recv.at[index], device[p][s])

    stores = []

    def store(at, count):
        rows = rows_at(at, count)
        copy = pltpu.make_async_copy(whole.at[rows], total_hbm.at[rows], store_sem.at[len(stores)])
        copy.start()
        stores.append(copy)

    small_copy = remote(small_mine.at[1 - core], small_got.at[0], small_send.at[0], small_recv.at[0], sibling)
    first = [None] * PARTS
    cube = [None] * PARTS

    def begin(p):
        first[p].wait_recv()
        at = away(p, 0)
        add_rows(work, at, work, at, from_core, at, size[1])
        cube[p] = scatter(p, 0)

    for p in range(PARTS):
        tiles(p, 1 - core)
        first[p] = core_piece(p, 0)
        tiles(p, core)
        if p > 0:
            begin(p - 1)
    second = [core_piece(p, 1) for p in range(PARTS)]
    begin(PARTS - 1)
    small_copy.wait_recv()
    small_held[0] = small_mine[core] + small_got[0]
    small_copy = remote(
        small_held.at[0], small_got.at[1], small_send.at[1], small_recv.at[1], {"replica": partners[0]}
    )
    for p in range(PARTS):
        second[p].wait_recv()
        at = held[p][1]
        add_rows(work, at, work, at, from_core, at, size[1])

    shared = [None] * PARTS
    for s in range(DIMS):
        later = [None] * PARTS
        for p in range(PARTS):
            copies = cube[p]
            copies[0].wait_recv()
            if s < DIMS - 1:
                at = away(p, s + 1)
                add_rows(work, at, work, at, from_cube, slot(p, s, 0), size[s + 2])
                later[p] = copies[1]
                cube[p] = scatter(p, s + 1)
            else:
                at = held[p][DIMS]
                add_rows(whole, at, work, at, from_cube, p * PART + PART - size[s], size[DIMS])
                shared[p] = {(s, 0): share(p, s, at, 0), (s - 1, 0): share(p, s - 1, at, 0)}
                store(at, size[DIMS])
        if s < DIMS - 1:
            for p in range(PARTS):
                later[p].wait_recv()
                at = held[p][s + 2]
                add_rows(work, at, work, at, from_cube, slot(p, s, 1), size[s + 2])
        small_copy.wait_recv()
        if s < DIMS - 1:
            small_held[s + 1] = small_held[s] + small_got[s + 1]
            small_copy = remote(
                small_held.at[s + 1], small_got.at[s + 2], small_send.at[s + 2], small_recv.at[s + 2],
                {"replica": partners[s + 1]},
            )
        else:
            small_out[...] = small_held[s] + small_got[s + 1]

    for s in reversed(range(DIMS)):
        for p in range(PARTS):
            shared[p][(s, 0)].wait_recv()
            if s < DIMS - 1:
                shared[p][(s, 1)].wait_recv()
            got = away(p, s)
            if s > 0:
                shared[p][(s - 1, 1)] = share(p, s - 1, got, 1)
            if s > 1:
                shared[p][(s - 2, 0)] = share(p, s - 2, held[p][s], 0)
            store(got, size[s + 1])

    for copy in sends:
        copy.wait_send()
    for copy in stores:
        copy.wait()
    output_copy.wait()
    gradient_copy.wait()


def specs(places):
    return [pl.BlockSpec(memory_space=place) for place in places]


def both_layers(operands, weights):
    dma = pltpu.SemaphoreType.DMA
    wide, narrow = pltpu.VMEM((TOKENS, WIDTH), F32), pltpu.VMEM((TOKENS, WIDTH), BF16)
    halves = pltpu.VMEM((2, 128, WIDTH), BF16)
    column = pltpu.VMEM((TOKENS, 16), F32)
    buffer = pltpu.VMEM((ROWS, COLS), BF16)
    inner = pltpu.VMEM((TOKENS, 1536), BF16)
    return pl.pallas_call(
        layer_kernel,
        out_shape=(
            jax.ShapeDtypeStruct((TOKENS, WIDTH), F32),
            jax.ShapeDtypeStruct((TOKENS, WIDTH), F32),
            jax.ShapeDtypeStruct((ROWS, COLS), BF16),
            jax.ShapeDtypeStruct((16, COLS), F32),
        ),
        in_specs=specs([pltpu.VMEM] * len(operands) + [pl.ANY] * len(weights)),
        out_specs=tuple(specs([pl.ANY, pl.ANY, pl.ANY, pltpu.VMEM])),
        scratch_shapes=[
            pltpu.VMEM((2, ROWS, COLS), BF16), buffer, buffer, buffer,
            pltpu.VMEM((2, 16, COLS), BF16), pltpu.VMEM((2, 16, COLS), F32),
            pltpu.VMEM((DIMS, 16, COLS), F32), pltpu.VMEM((DIMS + 1, 16, COLS), F32),
            halves, halves, halves, wide, pltpu.VMEM((2, 128, 128), F32), column, column,
            narrow, narrow, narrow, pltpu.VMEM((TOKENS, 512), BF16), pltpu.VMEM((TOKENS, 512), BF16),
            pltpu.VMEM((2, 8, 256, 128), BF16), narrow, wide, narrow, inner, inner, inner,
            narrow, pltpu.VMEM((TOKENS, 3072), BF16), narrow, pltpu.VMEM((TOKENS, 2048), BF16),
            wide, wide, narrow, wide,
            dma((18,)), dma((6,)), dma((6,)), dma, dma, dma((4,)), dma((4,)),
            dma((2 * PARTS,)), dma((2 * PARTS,)),
            dma((2 * PARTS * DIMS,)), dma((2 * PARTS * DIMS,)),
            dma((2 * PARTS * DIMS,)), dma((2 * PARTS * DIMS,)),
            dma((DIMS + 1,)), dma((DIMS + 1,)),
            dma((PARTS + PARTS * DIMS,)), dma((2,)),
        ],
        compiler_params=pltpu.CompilerParams(
            collective_id=1, has_side_effects=True, vmem_limit_bytes=VMEM_LIMIT
        ),
    )(*operands, *weights)


def unpack_kernel(
    total_ref, small_ref, output_ref, gradient_ref, mixer_ref, query_ref, key_ref, value_ref, out_ref,
    expert_ref, router_ref, gate_ref, up_ref, down_ref, output_out, gradient_out,
    got, wide, passed, load_sem, store_sem,
):
    loads = []
    for i in range(15):
        rows = pl.ds(i * 512, 512)
        copy = pltpu.make_async_copy(total_ref.at[rows], got.at[rows], load_sem.at[i])
        copy.start()
        loads.append(copy)
    passes = [
        pltpu.make_async_copy(source, passed.at[i], load_sem.at[15 + i])
        for i, source in enumerate((output_ref, gradient_ref))
    ]
    for copy in passes:
        copy.start()
    stores = []

    def send(source, target):
        copy = pltpu.make_async_copy(source, target, store_sem.at[len(stores)])
        copy.start()
        stores.append(copy)

    small = small_ref[...]
    mixer_ref[...] = small[0:1]
    expert_ref[...] = small[1:2]
    for i in range(3):
        router_ref[i] = small[2 + i:3 + i]

    def put(at, count, target):
        wide[at:at + count, :] = got[at:at + count, :].astype(F32)
        send(wide.at[pl.ds(at, count)], target)

    for i in range(15):
        loads[i].wait()
        at = i * 512
        cols = pl.ds((i % 2) * 512, 512)
        if i < 2:
            put(at, 512, query_ref.at[:, cols])
        elif i == 2:
            put(at, 512, key_ref)
        elif i == 3:
            put(at, 512, value_ref)
        elif i < 6:
            put(at, 512, out_ref.at[:, cols])
        elif i < 12:
            e, which = (i - 6) // 2, (i - 6) % 2
            put(at, 512, (up_ref if which else gate_ref).at[e])
        else:
            for j in range(2):
                put(at + j * 256, 256, down_ref.at[i - 12, :, pl.ds(j * 512, 512)])
    for i, target in enumerate((output_out, gradient_out)):
        passes[i].wait()
        send(passed.at[i], target)
    for copy in stores:
        copy.wait()


def unpack(total, small, output, gradient):
    shapes = (
        (1, 512), (512, 1024), (512, 512), (512, 512), (512, 1024), (1, 512), (3, 1, 512),
        (3, 512, 512), (3, 512, 512), (3, 256, 1024), (TOKENS, WIDTH), (TOKENS, WIDTH),
    )
    places = [pl.ANY if i not in (0, 5, 6) else pltpu.VMEM for i in range(12)]
    return pl.pallas_call(
        unpack_kernel,
        out_shape=tuple(jax.ShapeDtypeStruct(shape, F32) for shape in shapes),
        in_specs=specs([pl.ANY, pltpu.VMEM, pl.ANY, pl.ANY]),
        out_specs=tuple(specs(places)),
        scratch_shapes=[
            pltpu.VMEM((ROWS, COLS), BF16), pltpu.VMEM((ROWS, COLS), F32), pltpu.VMEM((2, TOKENS, WIDTH), F32),
            pltpu.SemaphoreType.DMA((17,)), pltpu.SemaphoreType.DMA((20,)),
        ],
        compiler_params=pltpu.CompilerParams(vmem_limit_bytes=VMEM_LIMIT),
    )(total, small, output, gradient)


def rotary_tables():
    lane = np.arange(256)
    frequency = np.power(10000.0, -2.0 * (lane % 32) / 64.0)
    angles = (np.arange(TOKENS) % 128)[:, None] * frequency[None, :]
    sign = np.where(lane % 64 < 32, -1.0, 1.0)[None, :]
    return np.cos(angles).astype(np.float32), (np.sin(angles) * sign).astype(np.float32)


def body(
    inputs, cotangent, segments, routes, mixer_gain, query_weight, key_matrix, value_matrix, out_weight,
    expert_gain, router_weight, gate_weight, up_weight, down_weight,
):
    cos, sin = (jnp.asarray(table) for table in rotary_tables())
    operands = (
        inputs.reshape(TOKENS, WIDTH), cotangent.reshape(TOKENS, WIDTH), segments.reshape(2, 128),
        jnp.swapaxes(routes[0, :, 0], 1, 2), mixer_gain, expert_gain, jnp.transpose(router_weight[0]), cos, sin,
    )
    weights = (
        query_weight[0], key_matrix[0], value_matrix[0], out_weight[0], gate_weight[0], up_weight[0],
        down_weight[0],
    )
    output, gradient, total, small = both_layers(operands, weights)
    *owned, output, gradient = unpack(total, small, output, gradient)
    return (
        output.reshape(1, 2, 1, 128, WIDTH),
        gradient.reshape(1, 2, 1, 128, WIDTH),
        owned[0],
    ) + tuple(item[None] for item in owned[1:5]) + (owned[5],) + (
        jnp.transpose(owned[6], (1, 2, 0)),
    ) + tuple(item[None] for item in owned[7:])


def solution(mesh):
    return jax.shard_map(
        body,
        mesh=mesh,
        in_specs=(
            P(None, ("shard", "replica"), None, None),
            P(None, ("shard", "replica"), None, None),
            P(None, ("shard", "replica"), None),
            P("section", None, ("shard", "replica"), None, None),
            P("section", "shard"),
            P("section", "shard", None),
            P("section", "shard", None),
            P("section", "shard", None),
            P("section", "shard", None),
            P("section", "shard"),
            P("section", "shard", None),
            P("section", None, "shard", None),
            P("section", None, "shard", None),
            P("section", None, "shard", None),
        ),
        out_specs=(
            P("section", None, ("shard", "replica"), None, None),
            P("section", None, ("shard", "replica"), None, None),
            P("section", "shard"),
            P("section", "shard", None),
            P("section", "shard", None),
            P("section", "shard", None),
            P("section", "shard", None),
            P("section", "shard"),
            P("section", "shard", None),
            P("section", None, "shard", None),
            P("section", None, "shard", None),
            P("section", None, "shard", None),
        ),
        check_vma=False,
    )
```

```python
import functools

import numpy as np
import jax
import jax.numpy as jnp
from jax import lax
from jax.experimental import pallas as pl
from jax.experimental.pallas import tpu as pltpu
from jax.sharding import PartitionSpec as P

EPSILON = 1e-06
NT = (((1,), (1,)), ((), ()))
NN = (((1,), (0,)), ((), ()))
TN = (((0,), (0,)), ((), ()))
F32 = jnp.float32
BF16 = jnp.bfloat16
TOKENS = 256
WIDTH = 1024
VMEM_LIMIT = 62 * 1024 * 1024
MESH = pl.DeviceIdType.MESH
ROWS = 7680
COLS = 512
PARTS = 5
PART = ROWS // PARTS
DIMS = 5
KEY, VALUE, OUT, EXPERT, DOWN = 1024, 1536, 2048, 3072, 6144
PIECES = ((0, 1024), (1024, 1024), (2048, 1024), (3072, 1536), (4608, 1536), (6144, 1536))


def dot(a, b, dims):
    return lax.dot_general(a, b, dims, preferred_element_type=F32)


def scale_of(rows):
    return lax.rsqrt(jnp.mean(rows * rows, axis=-1, keepdims=True) + EPSILON)


def swap_halves(u):
    lanes = u.shape[1]
    lane = lax.broadcasted_iota(jnp.int32, u.shape, 1)
    return jnp.where(lane % 64 < 32, pltpu.roll(u, lanes - 32, 1), pltpu.roll(u, 32, 1))


def low_half(shape):
    return lax.broadcasted_iota(jnp.int32, shape, 1) < 64


def both_ways(block):
    wide = block.astype(F32)
    turned = pltpu.roll(wide, 64, 1)
    low = low_half(wide.shape)
    return jnp.where(low, wide, turned).astype(BF16), jnp.where(low, turned, wide).astype(BF16)


def stack_heads(block):
    wide = block.astype(F32)
    low = low_half(wide.shape)
    zero = jnp.zeros_like(wide)
    return jnp.concatenate([jnp.where(low, wide, zero), jnp.where(low, zero, wide)], axis=0).astype(BF16)


def join_heads(rows):
    return jnp.where(low_half((128, 128)), rows[:128], rows[128:])


def norm_back(rows, scale, gain, incoming):
    weighted = incoming * gain
    gain_part = jnp.sum(incoming * rows * scale, axis=0, keepdims=True)
    part = scale * weighted - rows * (scale * scale * scale) * jnp.mean(weighted * rows, axis=-1, keepdims=True)
    return part, gain_part


def cube_position():
    r = lax.axis_index("replica")
    x = r % 4
    z = (r // 4) % 4
    y = r // 16
    bits = (((x + 1) // 2) % 2, x // 2, ((z + 1) // 2) % 2, z // 2, y)
    partners = (
        r + 1 - 2 * (x % 2),
        r + 3 - 2 * x,
        r + 4 - 8 * (z % 2),
        r + 12 - 8 * z,
        (r + 16) % 32,
    )
    return bits, partners


def rows_at(at, count):
    if isinstance(at, int):
        return pl.ds(at, count)
    return pl.ds(pl.multiple_of(at, 16), count)


def add_rows(dst, dst_at, a, b, b_at, count, lanes, b_lanes):
    step = min(count, 192)

    def one(i, carry):
        at = i * step
        dst[rows_at(dst_at + at, step), lanes] = (
            a[rows_at(dst_at + at, step), lanes] + b[rows_at(b_at + at, step), b_lanes]
        )
        return carry

    lax.fori_loop(0, count // step, one, 0)


def remote_copy(source, target, send_sem, recv_sem, device):
    return pltpu.make_async_remote_copy(
        src_ref=source, dst_ref=target, send_sem=send_sem, recv_sem=recv_sem,
        device_id=device, device_id_type=MESH,
    )


def layer_kernel(
    start_ref, loss_ref, segment_ref, route_ref, mixer_ref, expert_ref, router_ref, cos_ref, sin_ref,
    query_hbm, key_hbm, value_hbm, out_hbm, gate_hbm, up_hbm, down_hbm,
    output_hbm, gradient_hbm, total_hbm, small_out,
    pool, from_core, from_cube, whole, small_pair, small_mine, small_held, small_got,
    relayed, returned, relay, output, bias_ref, mark_ref, gate_ref,
    hidden_ref, normed_ref, q_ref, k_ref, v_ref, p_ref, att_ref, middle_ref, ne_ref, gl_ref, ul_ref, gi_ref,
    up_ref, bgu_ref, bb_ref, bqkv_ref, bne_ref, bm_ref, ba_ref, gradient,
    load_sem, weight_send, weight_recv, pair_send, pair_recv, relay_send, relay_recv,
    core_send, core_recv, cube_send, cube_recv, share_send, share_recv, small_send, small_recv, store_sem,
    output_sem,
):
    core = lax.axis_index("shard")
    section = lax.axis_index("section")
    bits, partners = cube_position()
    sibling = {"shard": 1 - core}
    other = {"section": 1 - section}

    barrier = pltpu.get_barrier_semaphore()
    pl.semaphore_signal(barrier, inc=1, device_id=sibling, device_id_type=MESH)
    pl.semaphore_signal(barrier, inc=1, device_id=other, device_id_type=MESH)
    for partner in partners:
        pl.semaphore_signal(barrier, inc=1, device_id={"replica": partner}, device_id_type=MESH)

    work = pool.at[core]
    loads = []

    def load(source, at, count):
        copy = pltpu.make_async_copy(source, work.at[pl.ds(at, count)], load_sem.at[len(loads)])
        copy.start()
        loads.append(copy)

    for i in range(2):
        load(query_hbm.at[:, pl.ds(i * 512, 512)], i * 512, 512)
    load(key_hbm, KEY, 512)
    load(value_hbm, VALUE, 512)
    for i in range(2):
        load(out_hbm.at[:, pl.ds(i * 512, 512)], OUT + i * 512, 512)
    for e in range(3):
        load(gate_hbm.at[e], EXPERT + e * 1024, 512)
        load(up_hbm.at[e], EXPERT + e * 1024 + 512, 512)
    for e in range(3):
        for i in range(2):
            load(down_hbm.at[e, :, pl.ds(i * 512, 512)], DOWN + e * 512 + i * 256, 256)
    needed = ((0, 1), (2, 3), (4, 5), (6, 7, 8), (9, 10, 11), (12, 13, 14, 15, 16, 17))

    pick = lax.broadcasted_iota(jnp.int32, (16, 3), 0) == lax.broadcasted_iota(jnp.int32, (16, 3), 1) + 2
    turned_router = dot(jnp.where(pick, 1.0, 0.0).astype(BF16), router_ref[...], NN)
    row = lax.broadcasted_iota(jnp.int32, (16, 512), 0)
    mixed = jnp.where(
        row == 0, mixer_ref[...].astype(F32), jnp.where(row == 1, expert_ref[...].astype(F32), turned_router)
    )
    small_pair[core] = mixed.astype(BF16)

    pl.semaphore_wait(barrier, 2 + DIMS)
    sends = []

    def remote(source, target, send_sem, recv_sem, device):
        copy = remote_copy(source, target, send_sem, recv_sem, device)
        copy.start()
        sends.append(copy)
        return copy

    pair = remote(small_pair.at[core], small_pair.at[core], pair_send, pair_recv, sibling)
    given = []
    for i, (at, count) in enumerate(PIECES):
        rows = pl.ds(at, count)
        given.append(
            remote_copy(work.at[rows], work.at[rows], weight_send.at[i], weight_recv.at[i], sibling)
        )

    def give(i):
        if i < len(PIECES):
            for index in needed[i]:
                loads[index].wait()
            given[i].start()

    def arrive(i):
        given[i].wait_recv()
        give(i + 2)

    give(0)
    give(1)

    position = lax.broadcasted_iota(jnp.int32, (128, 128), 0)
    earlier = lax.broadcasted_iota(jnp.int32, (128, 128), 1) <= position
    for pack in range(2):
        across = jnp.broadcast_to(segment_ref[pack:pack + 1, :].astype(F32), (128, 128))
        allowed = (across == jnp.transpose(across)) & earlier
        bias_ref[pack] = jnp.where(allowed, 0.0, -1e30)
    lane = lax.broadcasted_iota(jnp.int32, (TOKENS, 16), 1)
    expert_row = lax.broadcasted_iota(jnp.int32, (16, 128), 0)
    picked = []
    for pack in range(2):
        hit = (route_ref[pack, 0:1] + 2 == expert_row) | (route_ref[pack, 1:2] + 2 == expert_row)
        picked.append(jnp.transpose(jnp.where(hit, 1.0, 0.0)))
    marks = jnp.concatenate(picked, axis=0) > 0.0

    relays = [
        remote_copy(relay.at[i], relayed.at[i], relay_send.at[i], relay_recv.at[i], other) for i in range(2)
    ]
    returns = [
        remote_copy(relay.at[i], returned.at[i], relay_send.at[2 + i], relay_recv.at[2 + i], other)
        for i in range(2)
    ]

    pair.wait_recv()
    small = jnp.concatenate([small_pair[0], small_pair[1]], axis=1)
    mark_ref[...] = jnp.where(marks, 1.0, 0.0)

    def through(a_ref, part, at, lanes):
        return dot(a_ref[part, 0:512], pool[0, at:at + 512, lanes], NN) + dot(
            a_ref[part, 512:1024], pool[1, at:at + 512, lanes], NN
        )

    quarters = (slice(0, 256), slice(256, 512))

    def forward(part, ready):
        x = hidden_ref[part, :].astype(F32)
        normed_ref[part, :] = (x * scale_of(x) * small[0:1].astype(F32)).astype(BF16)

        for j, (target, at, turned) in enumerate(
            ((q_ref, 0, True), (q_ref, 512, True), (k_ref, 0, True), (v_ref, 0, False))
        ):
            if j % 2 == 0:
                ready(j // 2)
            for lanes in quarters:
                u = through(normed_ref, part, j * 512, lanes)
                if turned:
                    u = u * cos_ref[part, :] + swap_halves(u) * sin_ref[part, :]
                target[part, at + lanes.start:at + lanes.stop] = u.astype(BF16)

        for pack in range(part.start // 128, part.stop // 128):
            rows = slice(pack * 128, pack * 128 + 128)
            bias = jnp.concatenate([bias_ref[pack], bias_ref[pack]], axis=0)
            for pair_at in range(4):
                keys = both_ways(k_ref[rows, pair_at * 128:(pair_at + 1) * 128])
                values = both_ways(v_ref[rows, pair_at * 128:(pair_at + 1) * 128])
                for half in range(2):
                    g = pair_at * 2 + half
                    queries = stack_heads(q_ref[rows, g * 128:(g + 1) * 128])
                    scores = dot(queries, keys[half], NT) * 0.125 + bias
                    exponent = jnp.exp(scores - jnp.max(scores, axis=-1, keepdims=True))
                    attention = (exponent / jnp.sum(exponent, axis=-1, keepdims=True)).astype(BF16)
                    p_ref[pack, g] = attention
                    att_ref[rows, g * 128:(g + 1) * 128] = join_heads(dot(attention, values[half], NN)).astype(BF16)

        ready(2)
        for i in range(4):
            cols = slice(i * 256, (i + 1) * 256)
            middle_ref[part, cols] = hidden_ref[part, cols].astype(F32) + through(
                att_ref, part, OUT + (i // 2) * 512, quarters[i % 2]
            )
        middle = middle_ref[part, :]
        ne_ref[part, :] = (middle * scale_of(middle) * small[1:2].astype(F32)).astype(BF16)
        logits = dot(ne_ref[part, :], small, NT)
        marks = mark_ref[part, :] > 0.0
        peak = jnp.max(jnp.where(marks, logits, -1e30), axis=-1, keepdims=True)
        lifted = jnp.where(marks, jnp.exp(jnp.where(marks, logits - peak, 0.0)), 0.0)
        gates = lifted / jnp.sum(lifted, axis=-1, keepdims=True)
        gate_ref[part, :] = gates

        for e in range(3):
            if e < 2:
                ready(3 + e)
            for lanes in quarters:
                flat = slice(e * 512 + lanes.start, e * 512 + lanes.stop)
                gl = through(ne_ref, part, EXPERT + e * 1024, lanes)
                ul = through(ne_ref, part, EXPERT + e * 1024 + 512, lanes)
                gl_ref[part, flat] = gl.astype(BF16)
                ul_ref[part, flat] = ul.astype(BF16)
                inner = gl * jax.nn.sigmoid(gl) * ul
                gi_ref[part, flat] = (gates[:, 2 + e:3 + e] * inner).astype(BF16)

        ready(5)
        for i in range(4):
            cols = slice(i * 256, (i + 1) * 256)
            total = middle_ref[part, cols]
            for e in range(3):
                at = DOWN + e * 512 + (i // 2) * 256
                for h in range(2):
                    total = total + dot(
                        gi_ref[part, e * 512 + h * 256:e * 512 + (h + 1) * 256],
                        pool[h, at:at + 256, quarters[i % 2]], NN,
                    )
            output[part, cols] = total
            for pack in range(part.start // 128, part.stop // 128):
                at = pack * 128 - part.start
                relay[pack, :, cols] = total[at:at + 128].astype(BF16)

    @pl.when(section == 0)
    def _():
        hidden_ref[...] = start_ref[...]
        forward(slice(0, TOKENS), arrive)
        for pack in range(2):
            relays[pack].start()
            relays[pack].wait_send()

    @pl.when(section == 1)
    def _():
        for i in range(len(PIECES)):
            arrive(i)
        for pack in range(2):
            part = slice(pack * 128, pack * 128 + 128)
            relays[pack].wait_recv()
            hidden_ref[part, :] = relayed[pack]
            forward(part, lambda i: None)

    output_copy = pltpu.make_async_copy(output, output_hbm, output_sem.at[0])
    output_copy.start()

    cos, sin = cos_ref[0:128, 0:128], sin_ref[0:128, 0:128]

    def unturn(u):
        return (u * cos - swap_halves(u) * sin).astype(BF16)

    low = low_half((128, 128))
    def backward(part):
        gates = gate_ref[part, :]
        lane = lax.broadcasted_iota(jnp.int32, (128, 16), 1)
        pulls = jnp.zeros((128, 16), F32)
        for e in range(3):
            gate = gates[:, 2 + e:3 + e]
            for h in range(2):
                flat = slice(e * 512 + h * 256, e * 512 + (h + 1) * 256)
                at = DOWN + e * 512
                u = dot(up_ref[part, 0:512], pool[h, at:at + 256, :], NT) + dot(
                    up_ref[part, 512:1024], pool[h, at + 256:at + 512, :], NT
                )
                gl = gl_ref[part, flat].astype(F32)
                ul = ul_ref[part, flat].astype(F32)
                sg = jax.nn.sigmoid(gl)
                silu = gl * sg
                pulls = pulls + jnp.where(lane == 2 + e, jnp.sum(u * silu * ul, axis=-1, keepdims=True), 0.0)
                inner = gate * u
                at = e * 1024 + h * 256
                bgu_ref[part, at:at + 256] = (inner * ul * sg * (1.0 + gl * (1.0 - sg))).astype(BF16)
                bgu_ref[part, at + 512:at + 768] = (inner * silu).astype(BF16)
        back_logits = (gates * (pulls - jnp.sum(gates * pulls, axis=-1, keepdims=True))).astype(BF16)

        for i in range(4):
            cols = slice(i * 256, (i + 1) * 256)
            h, inside = i // 2, (i % 2) * 256
            total = dot(back_logits, small[:, cols], NN)
            for j in range(6):
                at = EXPERT + j * 512 + inside
                total = total + dot(bgu_ref[part, j * 512:(j + 1) * 512], pool[h, at:at + 256, :], NT)
            bne_ref[part, cols] = total
        middle = middle_ref[part, :]
        change, expert_gain = norm_back(middle, scale_of(middle), small[1:2].astype(F32), bne_ref[part, :])
        bm_ref[part, :] = up_ref[part, :].astype(F32) + change
        bb_ref[part, :] = bm_ref[part, :].astype(BF16)

        for i in range(4):
            h, inside = i // 2, (i % 2) * 256
            total = dot(bb_ref[part, 0:512], pool[h, OUT + inside:OUT + inside + 256, :], NT)
            total = total + dot(bb_ref[part, 512:1024], pool[h, OUT + 512 + inside:OUT + inside + 768, :], NT)
            ba_ref[part, i * 256:(i + 1) * 256] = total.astype(BF16)

        for pack in (part.start // 128,):
            rows = slice(pack * 128, pack * 128 + 128)
            for pair_at in range(4):
                keys = both_ways(k_ref[rows, pair_at * 128:(pair_at + 1) * 128])
                values = both_ways(v_ref[rows, pair_at * 128:(pair_at + 1) * 128])
                back_k, back_v = [], []
                for half in range(2):
                    g = pair_at * 2 + half
                    cols = slice(g * 128, (g + 1) * 128)
                    queries = stack_heads(q_ref[rows, cols])
                    back_out = stack_heads(ba_ref[rows, cols])
                    attention = p_ref[pack, g]
                    wide = attention.astype(F32)
                    pull = dot(back_out, values[half], NT)
                    bv = dot(attention, back_out, TN)
                    back_v.append(bv + pltpu.roll(bv, 64, 1))
                    spread = wide * pull
                    back_scores = (
                        (spread - wide * jnp.sum(spread, axis=-1, keepdims=True)) * 0.125
                    ).astype(BF16)
                    bqkv_ref[rows, cols] = unturn(join_heads(dot(back_scores, keys[half], NN)))
                    bk = dot(back_scores, queries, TN)
                    back_k.append(bk + pltpu.roll(bk, 64, 1))
                at = 1024 + pair_at * 128
                bqkv_ref[rows, at:at + 128] = unturn(jnp.where(low, back_k[0], back_k[1]))
                bqkv_ref[rows, at + 512:at + 640] = jnp.where(low, back_v[0], back_v[1]).astype(BF16)

        for i in range(4):
            h, inside = i // 2, (i % 2) * 256
            total = jnp.zeros((128, 256), F32)
            for j in range(4):
                at = j * 512 + inside
                total = total + dot(bqkv_ref[part, j * 512:(j + 1) * 512], pool[h, at:at + 256, :], NT)
            bne_ref[part, i * 256:(i + 1) * 256] = total
        x = hidden_ref[part, :].astype(F32)
        change, mixer_gain = norm_back(x, scale_of(x), small[0:1].astype(F32), bne_ref[part, :])
        gradient[part, :] = bm_ref[part, :] + change
        relay[part.start // 128] = gradient[part, :].astype(BF16)
        router = dot(back_logits, ne_ref[part, :], TN)
        row = lax.broadcasted_iota(jnp.int32, router.shape, 0)
        return jnp.where(row == 0, mixer_gain, jnp.where(row == 1, expert_gain, router))

    mixed = jnp.zeros((16, WIDTH), F32)
    for pack in range(2):
        part = slice(pack * 128, pack * 128 + 128)

        @pl.when(section == 0)
        def _():
            returns[pack].wait_recv()
            up_ref[part, :] = returned[pack]

        @pl.when(section == 1)
        def _():
            up_ref[part, :] = loss_ref[part, :]

        mixed = mixed + backward(part)

        @pl.when(section == 1)
        def _():
            returns[pack].start()

    gradient_copy = pltpu.make_async_copy(gradient, gradient_hbm, output_sem.at[1])
    gradient_copy.start()
    small_mine[0] = mixed[:, 0:512]
    small_mine[1] = mixed[:, 512:1024]

    def tiles(p, half, lanes_at):
        lanes = pl.ds(pl.multiple_of(lanes_at, 256), 256)

        def tile(a, a_at, count, b, b_at, at):
            rows = a[:, pl.ds(pl.multiple_of(a_at, 256), count)]
            columns = b[:, pl.ds(pl.multiple_of(b_at + lanes_at, 256), 256)]
            pool[half, at:at + count, lanes] = dot(rows, columns, TN).astype(BF16)

        left = half * 512
        if p == 0:
            for i in range(3):
                tile(normed_ref, left, 512, bqkv_ref, i * 512, i * 512)
        elif p == 1:
            tile(normed_ref, left, 512, bqkv_ref, 1536, VALUE)
            for i in range(2):
                tile(att_ref, left, 512, bb_ref, i * 512, OUT + i * 512)
        elif p < 4:
            for i in range(3 * p - 6, 3 * p - 3):
                tile(ne_ref, left, 512, bgu_ref, i * 512, EXPERT + i * 512)
        else:
            for e in range(3):
                for i in range(2):
                    tile(gi_ref, e * 512 + half * 256, 256, up_ref, i * 512, DOWN + e * 512 + i * 256)

    for copy in given + [pair]:
        copy.wait_send()
    sends.clear()

    @pl.when(section == 1)
    def _():
        for i in range(2):
            returns[i].wait_send()

    lent = pool.at[1 - core]
    size = [PART] + [PART >> s for s in range(DIMS)]
    bit = [[bits[(p + s) % DIMS] for s in range(DIMS)] for p in range(PARTS)]
    device = [[{"replica": partners[(p + s) % DIMS]} for s in range(DIMS)] for p in range(PARTS)]
    base = [p * PART for p in range(PARTS)]
    held = [[at, at] for at in base]
    for p in range(PARTS):
        for s in range(1, DIMS):
            held[p].append(held[p][s] + bit[p][s] * size[s + 1])
    kept_at = [bit[p][0] * 256 for p in range(PARTS)]
    sent_at = [256 - at for at in kept_at]
    kept = [pl.ds(pl.multiple_of(at, 256), 256) for at in kept_at]
    sent = [pl.ds(pl.multiple_of(at, 256), 256) for at in sent_at]
    sides = (slice(0, 256),) + (slice(256, 512),) * (DIMS - 1)

    def away(p, s):
        return held[p][s] + (1 - bit[p][s]) * size[s + 1]

    def core_piece(p, piece):
        place = (pl.ds(base[p], PART), kept[p] if piece else sent[p])
        return remote(
            lent.at[place], from_core.at[place], core_send.at[2 * p + piece], core_recv.at[2 * p + piece], sibling
        )

    def slot(p, s, piece):
        at = base[p] + PART - size[s]
        return at + piece * size[s + 2] if piece else at

    def scatter(p, s):
        copies = []
        for piece in range(2 if s < DIMS - 1 else 1):
            index = (p * DIMS + s) * 2 + piece
            at = away(p, s) if s > 0 else base[p]
            count = size[s + 1]
            if s < DIMS - 1:
                b = bit[p][s + 1]
                count = size[s + 2]
                at = at + ((1 - b) if piece == 0 else b) * count
            side = sides[s]
            copies.append(remote(
                work.at[rows_at(at, count), kept[p] if s > 0 else sent[p]],
                from_cube.at[rows_at(slot(p, s, piece), count), pl.ds(side.start, 256)],
                cube_send.at[index], cube_recv.at[index], device[p][s],
            ))
        return copies

    def share(p, s, at, piece):
        count = size[s + 2] if s < DIMS - 1 else size[DIMS]
        index = (p * DIMS + s) * 2 + piece
        place = (rows_at(at, count), kept[p])
        return remote(whole.at[place], whole.at[place], share_send.at[index], share_recv.at[index], device[p][s])

    stores = []

    def store(at, count, lanes):
        place = (rows_at(at, count), lanes)
        copy = pltpu.make_async_copy(whole.at[place], total_hbm.at[place], store_sem.at[len(stores)])
        copy.start()
        stores.append(copy)

    small_copy = remote(small_mine.at[1 - core], small_got.at[0], small_send.at[0], small_recv.at[0], sibling)
    first = [None] * PARTS
    second = [None] * PARTS
    cube = [None] * PARTS
    for p in range(PARTS):
        tiles(p, 1 - core, sent_at[p])
        first[p] = core_piece(p, 0)
    for p in range(PARTS):
        tiles(p, core, sent_at[p])
        first[p].wait_recv()
        add_rows(work, base[p], work, from_core, base[p], PART, sent[p], sent[p])
        cube[p] = scatter(p, 0)
    for p in range(PARTS):
        tiles(p, 1 - core, kept_at[p])
        second[p] = core_piece(p, 1)
    for p in range(PARTS):
        tiles(p, core, kept_at[p])
    small_copies = [small_copy]

    def small_hop(s):
        small_copies.append(remote(
            small_held.at[s], small_got.at[s + 1], small_send.at[s + 1], small_recv.at[s + 1],
            {"replica": partners[s]},
        ))

    def small_step(s):
        small_copies[-1].wait_recv()
        if s < DIMS - 1:
            small_held[s + 1] = small_held[s] + small_got[s + 1]
            small_hop(s + 1)
        else:
            small_out[...] = small_held[s] + small_got[s + 1]

    small_copy.wait_recv()
    small_held[0] = small_mine[core] + small_got[0]
    small_hop(0)
    for p in range(PARTS):
        second[p].wait_recv()
        add_rows(work, base[p], work, from_core, base[p], PART, kept[p], kept[p])

    shared = [None] * PARTS
    for s in range(DIMS):
        later = [None] * PARTS
        for p in range(PARTS):
            copies = cube[p]
            copies[0].wait_recv()
            if s < DIMS - 1:
                at = away(p, s + 1)
                add_rows(work, at, work, from_cube, slot(p, s, 0), size[s + 2], kept[p], sides[s])
                later[p] = copies[1]
                cube[p] = scatter(p, s + 1)
            else:
                at = held[p][DIMS]
                add_rows(whole, at, work, from_cube, slot(p, s, 0), size[DIMS], kept[p], sides[s])
                shared[p] = {(s, 0): share(p, s, at, 0), (s - 1, 0): share(p, s - 1, at, 0)}
                store(at, size[DIMS], kept[p])
        if s < DIMS - 1:
            for p in range(PARTS):
                later[p].wait_recv()
                at = held[p][s + 2]
                add_rows(work, at, work, from_cube, slot(p, s, 1), size[s + 2], kept[p], sides[s])
        if s < 2:
            small_step(s)

    for s in reversed(range(DIMS)):
        for p in range(PARTS):
            shared[p][(s, 0)].wait_recv()
            if s < DIMS - 1:
                shared[p][(s, 1)].wait_recv()
            if s > 0:
                got = away(p, s)
                shared[p][(s - 1, 1)] = share(p, s - 1, got, 1)
                store(got, size[s + 1], kept[p])
            else:
                store(base[p], PART, sent[p])
            if s > 1:
                shared[p][(s - 2, 0)] = share(p, s - 2, held[p][s], 0)
        if s < 3:
            small_step(DIMS - 1 - s)

    for copy in sends:
        copy.wait_send()
    for copy in stores:
        copy.wait()
    output_copy.wait()
    gradient_copy.wait()


def specs(places):
    return [pl.BlockSpec(memory_space=place) for place in places]


def both_layers(operands, weights):
    dma = pltpu.SemaphoreType.DMA
    wide, narrow = pltpu.VMEM((TOKENS, WIDTH), F32), pltpu.VMEM((TOKENS, WIDTH), BF16)
    halves = pltpu.VMEM((2, 128, WIDTH), BF16)
    column = pltpu.VMEM((TOKENS, 16), F32)
    buffer = pltpu.VMEM((ROWS, COLS), BF16)
    inner = pltpu.VMEM((TOKENS, 1536), BF16)
    return pl.pallas_call(
        layer_kernel,
        out_shape=(
            jax.ShapeDtypeStruct((TOKENS, WIDTH), F32),
            jax.ShapeDtypeStruct((TOKENS, WIDTH), F32),
            jax.ShapeDtypeStruct((ROWS, COLS), BF16),
            jax.ShapeDtypeStruct((16, COLS), F32),
        ),
        in_specs=specs([pltpu.VMEM] * len(operands) + [pl.ANY] * len(weights)),
        out_specs=tuple(specs([pl.ANY, pl.ANY, pl.ANY, pltpu.VMEM])),
        scratch_shapes=[
            pltpu.VMEM((2, ROWS, COLS), BF16), buffer, buffer, buffer,
            pltpu.VMEM((2, 16, COLS), BF16), pltpu.VMEM((2, 16, COLS), F32),
            pltpu.VMEM((DIMS, 16, COLS), F32), pltpu.VMEM((DIMS + 1, 16, COLS), F32),
            halves, halves, halves, wide, pltpu.VMEM((2, 128, 128), F32), column, column,
            narrow, narrow, narrow, pltpu.VMEM((TOKENS, 512), BF16), pltpu.VMEM((TOKENS, 512), BF16),
            pltpu.VMEM((2, 8, 256, 128), BF16), narrow, wide, narrow, inner, inner, inner,
            narrow, pltpu.VMEM((TOKENS, 3072), BF16), narrow, pltpu.VMEM((TOKENS, 2048), BF16),
            wide, wide, narrow, wide,
            dma((18,)), dma((6,)), dma((6,)), dma, dma, dma((4,)), dma((4,)),
            dma((2 * PARTS,)), dma((2 * PARTS,)),
            dma((2 * PARTS * DIMS,)), dma((2 * PARTS * DIMS,)),
            dma((2 * PARTS * DIMS,)), dma((2 * PARTS * DIMS,)),
            dma((DIMS + 1,)), dma((DIMS + 1,)),
            dma((PARTS + PARTS * DIMS,)), dma((2,)),
        ],
        compiler_params=pltpu.CompilerParams(
            collective_id=1, has_side_effects=True, vmem_limit_bytes=VMEM_LIMIT
        ),
    )(*operands, *weights)


def unpack_kernel(
    total_ref, small_ref, output_ref, gradient_ref, mixer_ref, query_ref, key_ref, value_ref, out_ref,
    expert_ref, router_ref, gate_ref, up_ref, down_ref, output_out, gradient_out,
    got, wide, passed, load_sem, store_sem,
):
    loads = []
    for i in range(15):
        rows = pl.ds(i * 512, 512)
        copy = pltpu.make_async_copy(total_ref.at[rows], got.at[rows], load_sem.at[i])
        copy.start()
        loads.append(copy)
    passes = [
        pltpu.make_async_copy(source, passed.at[i], load_sem.at[15 + i])
        for i, source in enumerate((output_ref, gradient_ref))
    ]
    for copy in passes:
        copy.start()
    stores = []

    def send(source, target):
        copy = pltpu.make_async_copy(source, target, store_sem.at[len(stores)])
        copy.start()
        stores.append(copy)

    small = small_ref[...]
    mixer_ref[...] = small[0:1]
    expert_ref[...] = small[1:2]
    for i in range(3):
        router_ref[i] = small[2 + i:3 + i]

    def put(at, count, target):
        wide[at:at + count, :] = got[at:at + count, :].astype(F32)
        send(wide.at[pl.ds(at, count)], target)

    for i in range(15):
        loads[i].wait()
        at = i * 512
        cols = pl.ds((i % 2) * 512, 512)
        if i < 2:
            put(at, 512, query_ref.at[:, cols])
        elif i == 2:
            put(at, 512, key_ref)
        elif i == 3:
            put(at, 512, value_ref)
        elif i < 6:
            put(at, 512, out_ref.at[:, cols])
        elif i < 12:
            e, which = (i - 6) // 2, (i - 6) % 2
            put(at, 512, (up_ref if which else gate_ref).at[e])
        else:
            for j in range(2):
                put(at + j * 256, 256, down_ref.at[i - 12, :, pl.ds(j * 512, 512)])
    for i, target in enumerate((output_out, gradient_out)):
        passes[i].wait()
        send(passed.at[i], target)
    for copy in stores:
        copy.wait()


def unpack(total, small, output, gradient):
    shapes = (
        (1, 512), (512, 1024), (512, 512), (512, 512), (512, 1024), (1, 512), (3, 1, 512),
        (3, 512, 512), (3, 512, 512), (3, 256, 1024), (TOKENS, WIDTH), (TOKENS, WIDTH),
    )
    places = [pl.ANY if i not in (0, 5, 6) else pltpu.VMEM for i in range(12)]
    return pl.pallas_call(
        unpack_kernel,
        out_shape=tuple(jax.ShapeDtypeStruct(shape, F32) for shape in shapes),
        in_specs=specs([pl.ANY, pltpu.VMEM, pl.ANY, pl.ANY]),
        out_specs=tuple(specs(places)),
        scratch_shapes=[
            pltpu.VMEM((ROWS, COLS), BF16), pltpu.VMEM((ROWS, COLS), F32), pltpu.VMEM((2, TOKENS, WIDTH), F32),
            pltpu.SemaphoreType.DMA((17,)), pltpu.SemaphoreType.DMA((20,)),
        ],
        compiler_params=pltpu.CompilerParams(vmem_limit_bytes=VMEM_LIMIT),
    )(total, small, output, gradient)


def rotary_tables():
    lane = np.arange(256)
    frequency = np.power(10000.0, -2.0 * (lane % 32) / 64.0)
    angles = (np.arange(TOKENS) % 128)[:, None] * frequency[None, :]
    sign = np.where(lane % 64 < 32, -1.0, 1.0)[None, :]
    return np.cos(angles).astype(np.float32), (np.sin(angles) * sign).astype(np.float32)


def body(
    inputs, cotangent, segments, routes, mixer_gain, query_weight, key_matrix, value_matrix, out_weight,
    expert_gain, router_weight, gate_weight, up_weight, down_weight,
):
    cos, sin = (jnp.asarray(table) for table in rotary_tables())
    operands = (
        inputs.reshape(TOKENS, WIDTH), cotangent.reshape(TOKENS, WIDTH), segments.reshape(2, 128),
        jnp.swapaxes(routes[0, :, 0], 1, 2), mixer_gain, expert_gain, jnp.transpose(router_weight[0]), cos, sin,
    )
    weights = (
        query_weight[0], key_matrix[0], value_matrix[0], out_weight[0], gate_weight[0], up_weight[0],
        down_weight[0],
    )
    output, gradient, total, small = both_layers(operands, weights)
    *owned, output, gradient = unpack(total, small, output, gradient)
    return (
        output.reshape(1, 2, 1, 128, WIDTH),
        gradient.reshape(1, 2, 1, 128, WIDTH),
        owned[0],
    ) + tuple(item[None] for item in owned[1:5]) + (owned[5],) + (
        jnp.transpose(owned[6], (1, 2, 0)),
    ) + tuple(item[None] for item in owned[7:])


def solution(mesh):
    return jax.shard_map(
        body,
        mesh=mesh,
        in_specs=(
            P(None, ("shard", "replica"), None, None),
            P(None, ("shard", "replica"), None, None),
            P(None, ("shard", "replica"), None),
            P("section", None, ("shard", "replica"), None, None),
            P("section", "shard"),
            P("section", "shard", None),
            P("section", "shard", None),
            P("section", "shard", None),
            P("section", "shard", None),
            P("section", "shard"),
            P("section", "shard", None),
            P("section", None, "shard", None),
            P("section", None, "shard", None),
            P("section", None, "shard", None),
        ),
        out_specs=(
            P("section", None, ("shard", "replica"), None, None),
            P("section", None, ("shard", "replica"), None, None),
            P("section", "shard"),
            P("section", "shard", None),
            P("section", "shard", None),
            P("section", "shard", None),
            P("section", "shard", None),
            P("section", "shard"),
            P("section", "shard", None),
            P("section", None, "shard", None),
            P("section", None, "shard", None),
            P("section", None, "shard", None),
        ),
        check_vma=False,
    )
```
